32 devices in a mesh: groups: 2 (over x), depth: 16 (over z, y, core).
Axes of the slice: x: 2, y: 2, z: 4, core: 2. Of those that a mesh axis runs over, the one named last changes fastest.
Arguments:
- alignment_token_grid: int32 [64, 256], P(('groups', 'depth')), parts along dimension 0, may hold values from 0 to 32
- residue_chain_index: int32 [512], P('groups'), parts along dimension 0, may hold values from 0 to 1, as said below
- alignment_state: bfloat16 [64, 256, 768], P(('groups', 'depth')), parts along dimension 0, may hold values from -6 to 6
- embedding: bfloat16 [33, 768], replicated, may hold values from -6 to 6
- chain_head_bias: float32 [2, 12], replicated, may hold values from -2 to 2
- row_query_key_value: bfloat16 [768, 2304], replicated
- row_output_weight: bfloat16 [768, 768], replicated, may hold values from -0.21875 to 0.21875
- column_query_key_value: bfloat16 [768, 2304], replicated
- column_output_weight: bfloat16 [768, 768], replicated, may hold values from -0.21875 to 0.21875
- feed_up_weight: bfloat16 [768, 3072], P('depth'), may hold values from -0.21875 to 0.21875
- feed_down_weight: bfloat16 [3072, 768], P('depth'), may hold values from -0.109375 to 0.109375
Outputs:
- layer_out: bfloat16 [64, 256, 768], P('groups', 'depth'), parts along dimension 0
The draws below stay inside these ranges and needn't reach their ends.
There are 2 independent parts, one for each index of `groups`. The reference program is written for one: setup_inputs(seed, part) draws one part's arguments, and reference() takes and returns one part's arrays. A program takes and returns all parts, laid end to end along the dimension named above; an argument that names none is the same for every part. Nothing has to cross between parts.
Inputs may be any that keep to these rules, and one draw needn't show every extreme that they name: `residue_chain_index`: the residues of the first chain come first, then those of the second; each chain holds 64 to 192 residues.
All inputs are finite; a program needn't handle non-finite values.
Results may differ from the reference program's by a relative error of at most 0.007.
Values may be sent and summed in bfloat16 or wider, within the bound.
A program may use at most 128 MiB of HBM per device.

```python
import math
import jax
import jax.numpy as jnp
import numpy as np
from jax import lax

MODEL_WIDTH = 768
H = 12
FF = 3072
TOKEN_ALPHABET = 33
HEAD = 64
RESIDUE_COUNT = 256
SEQUENCE_COUNT = 32


def projection(key):
    base = jax.random.normal(key, (MODEL_WIDTH, 3, H, HEAD), jnp.float32) * MODEL_WIDTH ** (-0.5)
    keys_part = base[:, 1]
    stacked = jnp.stack([base[:, 0], keys_part, base[:, 2]], axis=1)
    return stacked.reshape(MODEL_WIDTH, 3 * MODEL_WIDTH).astype(jnp.bfloat16)


def draw_row_query_key_value(key, part):
    key = jax.random.fold_in(key, 11)
    return projection(key)


def draw_column_query_key_value(key, part):
    key = jax.random.fold_in(key, 23)
    return projection(key)


def draw_residue_chain_index(key, part):
    key = jax.random.fold_in(key, 37)
    cut = jax.random.randint(key, (), RESIDUE_COUNT // 4, 3 * RESIDUE_COUNT // 4 + 1)
    return (jnp.arange(RESIDUE_COUNT, dtype=jnp.int32) >= cut).astype(jnp.int32)


def plant(values, key, least, high):
    longest = values.shape.index(max(values.shape))
    spots = []
    for shift in (0, 1):
        where = [jax.random.randint(jax.random.fold_in(key, axis), (), 0, length) for axis, length in enumerate(values.shape)]
        where[longest] = (where[longest] + shift) % values.shape[longest]
        spots.append(tuple(where))
    return values.at[spots[0]].set(least).at[spots[1]].set(high)


def with_spikes(values, key, source, target, parts, factor):
    def block_of(position):
        return (jnp.arange(values.shape[position]) // (values.shape[position] // parts)).reshape((-1,) + (1,) * (values.ndim - 1 - position))

    near = jax.random.permutation(key, parts)[block_of(target)]
    second = (block_of(target) + parts // 2) % parts
    return jnp.where((block_of(source) == near) | (block_of(source) == second), factor * values, values)


def levels(rng, dims, cuts, low, largest):
    gain, own = 1.0, jax.random.fold_in(rng, 6)
    for dim, shards_of in cuts:
        draws = jnp.exp(jax.random.uniform(jax.random.fold_in(own, dim), (shards_of,), jnp.float32, low / len(cuts), largest / len(cuts)))
        gain = gain * jnp.repeat(draws, dims[dim] // shards_of).reshape([-1 if axis == dim else 1 for axis in range(len(dims))])
    return gain


def cumulative_ranks(count, skew):
    weights = [(1 << 20) // math.isqrt(standing ** skew) + 1 for standing in range(1, count + 1)]
    deviation = 1 + sum(weights) // (1 << 30)
    return np.cumsum(np.array([max(1, weight // deviation) for weight in weights]))


def ranked(key, extent, number_of, skew):
    grid = cumulative_ranks(number_of, skew)
    pick = jax.random.randint(jax.random.fold_in(key, 1), extent, 0, int(grid[number_of - 1]))
    standing = jnp.searchsorted(jnp.asarray(grid, jnp.int32), pick, side="right")
    return jax.random.permutation(jax.random.fold_in(key, 2), number_of)[standing].astype(jnp.int32)


def normal_values(key, dims, deviation, bound, pieces=(), kind=jnp.bfloat16):
    gain = levels(key, dims, pieces, -0.22, 0.18) if pieces else 1.0
    array = jax.random.normal(key, dims, jnp.float32) * deviation * gain
    return jnp.minimum(jnp.maximum(array, -bound), bound).astype(kind)


def bell_draw_with(own_key, shape, scale, most, shards, heavy, held_as=jnp.bfloat16):
    array = scale * jax.random.normal(own_key, shape, jnp.float32)
    if shards:
        array = array * levels(own_key, shape, shards, -0.22, 0.18)
    return jnp.clip(with_spikes(array, jax.random.fold_in(own_key, 3), *heavy), -most, most).astype(held_as)


def setup_inputs(seed: int = 0, part: int = 0) -> dict:
    key_of = jax.random.split(jax.random.key(seed), 12)
    own_keys = jax.random.split(jax.random.fold_in(key_of[11], part), 12)
    return {
        "alignment_token_grid": plant(ranked(own_keys[0], (SEQUENCE_COUNT, RESIDUE_COUNT), TOKEN_ALPHABET, 2), jax.random.fold_in(own_keys[0], 3), 0, TOKEN_ALPHABET - 1).astype(jnp.int32),
        "residue_chain_index": draw_residue_chain_index(jax.random.fold_in(jax.random.fold_in(key_of[11], part), 71), part),
        "alignment_state": bell_draw_with(own_keys[2], (SEQUENCE_COUNT, RESIDUE_COUNT, MODEL_WIDTH), 1.0, 6.0, ((0, 16),), (0, 1, 16, 2.0)),
        "embedding": normal_values(key_of[3], (TOKEN_ALPHABET, MODEL_WIDTH), 1.0, 6.0),
        "chain_head_bias": jnp.clip(jax.random.uniform(key_of[4], (2, H), jnp.float32, -2.0, 2.0), -2.0, 2.0),
        "row_query_key_value": draw_row_query_key_value(jax.random.fold_in(key_of[11], 71), part),
        "row_output_weight": normal_values(key_of[6], (MODEL_WIDTH, MODEL_WIDTH), MODEL_WIDTH ** -0.5, 0.21875),
        "column_query_key_value": draw_column_query_key_value(jax.random.fold_in(key_of[11], 71), part),
        "column_output_weight": normal_values(key_of[8], (MODEL_WIDTH, MODEL_WIDTH), MODEL_WIDTH ** -0.5, 0.21875),
        "feed_up_weight": normal_values(key_of[9], (MODEL_WIDTH, FF), MODEL_WIDTH ** -0.5, 0.21875, ((0, 16),)),
        "feed_down_weight": normal_values(key_of[10], (FF, MODEL_WIDTH), FF ** -0.5, 0.109375, ((0, 16),)),
    }


def layer_norm(values):
    values = values.astype(jnp.float32)
    center = values - lax.optimization_barrier(jnp.mean(values, axis=-1, keepdims=True))
    spread = lax.optimization_barrier(jnp.mean(center * center, axis=-1, keepdims=True))
    return center * lax.rsqrt(spread + 1e-05)

def reference(alignment_token_grid, residue_chain_index, alignment_state, embedding, chain_head_bias, row_query_key_value, row_output_weight, column_query_key_value, column_output_weight, feed_up_weight, feed_down_weight):
    sequence_total = alignment_state.shape[0]
    residue_length = alignment_state.shape[1]
    initial_input0 = alignment_state.astype(jnp.float32) + embedding[alignment_token_grid].astype(jnp.float32)
    u1 = layer_norm(initial_input0).astype(jnp.bfloat16)
    qkv1 = jnp.dot(u1.reshape(sequence_total * residue_length, MODEL_WIDTH), row_query_key_value, preferred_element_type=jnp.float32).astype(jnp.bfloat16)
    qkv1 = qkv1.reshape(sequence_total, residue_length, 3, H, HEAD).astype(jnp.float32)
    tied = jnp.einsum('sihd,sjhd->ihj', qkv1[:, :, 0], qkv1[:, :, 1]) / (math.sqrt(HEAD) * math.sqrt(sequence_total))
    same = residue_chain_index[:, None] == residue_chain_index[None, :]
    tied = tied + jnp.where(same[:, None, :], chain_head_bias[1][None, :, None], chain_head_bias[0][None, :, None])
    row_probs = jax.nn.softmax(tied, axis=-1).astype(jnp.bfloat16)
    row_mix = jnp.einsum('ihj,sjhd->sihd', row_probs.astype(jnp.float32), qkv1[:, :, 2]).astype(jnp.bfloat16)
    x1 = initial_input0.reshape(sequence_total * residue_length, MODEL_WIDTH) + jnp.dot(row_mix.reshape(sequence_total * residue_length, MODEL_WIDTH), row_output_weight, preferred_element_type=jnp.float32)
    x1 = x1.astype(jnp.bfloat16).reshape(sequence_total, residue_length, MODEL_WIDTH)
    columns = jnp.transpose(x1, (1, 0, 2)).reshape(residue_length // 8, 8, sequence_total, MODEL_WIDTH)

    def column_block(block):
        hidden_width = block.shape[0]
        flat = block.reshape(hidden_width * sequence_total, MODEL_WIDTH).astype(jnp.float32)
        u2 = layer_norm(flat).astype(jnp.bfloat16)
        qkv2 = jnp.dot(u2, column_query_key_value, preferred_element_type=jnp.float32).astype(jnp.bfloat16)
        qkv2 = qkv2.reshape(hidden_width, sequence_total, 3, H, HEAD).astype(jnp.float32)
        scores = jnp.einsum('nshd,nthd->nhst', qkv2[:, :, 0], qkv2[:, :, 1]) / math.sqrt(HEAD)
        col_probs = jax.nn.softmax(scores, axis=-1).astype(jnp.bfloat16)
        col_mix = jnp.einsum('nhst,nthd->nshd', col_probs.astype(jnp.float32), qkv2[:, :, 2]).astype(jnp.bfloat16)
        x2 = flat + jnp.dot(col_mix.reshape(hidden_width * sequence_total, MODEL_WIDTH), column_output_weight, preferred_element_type=jnp.float32)
        u3 = layer_norm(x2).astype(jnp.bfloat16)
        hidden = jax.nn.gelu(jnp.dot(u3, feed_up_weight, preferred_element_type=jnp.float32), approximate=False).astype(jnp.bfloat16)
        result = x2 + jnp.dot(hidden, feed_down_weight, preferred_element_type=jnp.float32)
        return result.astype(jnp.bfloat16).reshape(hidden_width, sequence_total, MODEL_WIDTH)
    done = lax.map(column_block, columns).reshape(residue_length, sequence_total, MODEL_WIDTH)
    return jnp.transpose(done, (1, 0, 2))
```

```python
import functools
import math

import jax
import jax.numpy as jnp
from jax import lax
from jax.experimental import pallas as pl
from jax.experimental.pallas import tpu as pltpu
from jax.sharding import PartitionSpec as P

MESH = pl.DeviceIdType.MESH
BF = jnp.bfloat16
F32 = jnp.float32


def dot(a, b):
    return jnp.dot(a, b, preferred_element_type=F32)


def dot_t(a, b):
    return lax.dot_general(a, b, (((1,), (1,)), ((), ())), preferred_element_type=F32)


def half_masks(width):
    lane = lax.broadcasted_iota(jnp.int32, (1, width), 1)
    low = jnp.where(lane < width // 2, 1.0, 0.0)
    return low.astype(BF), (1.0 - low).astype(BF)


def project_into(source, weight_ref, target_ref, step):
    def body(t, carry):
        cols = pl.ds(pl.multiple_of(t * step, step), step)
        target_ref[:, cols] = dot(source, weight_ref[:, cols]).astype(BF)
        return carry

    lax.fori_loop(0, weight_ref.shape[1] // step, body, 0)


def row_kernel(
    n, seqs, length, heads, head_size,
    tok_ref, chain_col, chain_row, state_ref, emb_ref, bias_ref, wqkv_ref, wo_ref,
    out_ref,
    x0_ref, qkv_ref, sbuf, rbuf, tbuf, gbuf, pbuf, mix_ref, xbuf,
    pair_sems, rs_send, rs_recv, ag_send, ag_recv, fw_send, fw_recv, aa_send, aa_recv, local_sem,
):
    me = lax.axis_index("depth")
    core = lax.rem(me, 2)
    chip = me // 2
    chips = n // 2
    sibling = me + 1 - 2 * core
    share = length // n
    width = heads * head_size

    barrier = pltpu.get_barrier_semaphore()

    def greet(k, carry):
        pl.semaphore_signal(
            barrier, inc=1, device_id={"depth": lax.rem(me + k, n)}, device_id_type=MESH
        )
        return carry

    lax.fori_loop(1, n, greet, 0)

    letters = lax.broadcasted_iota(jnp.int32, (seqs * length, emb_ref.shape[0]), 1)
    one_hot = jnp.where(tok_ref[...] == letters, 1.0, 0.0).astype(BF)
    x0_ref[...] = state_ref[...].astype(F32) + dot(one_hot, emb_ref[...])
    u1 = layer_norm(x0_ref[...]).astype(BF)
    project_into(u1, wqkv_ref, qkv_ref, 256)
    low, high = half_masks(2 * head_size)

    def pair_cols(which, p):
        cols = pl.ds(pl.multiple_of(which * width + p * 2 * head_size, 2 * head_size), 2 * head_size)
        return [qkv_ref[pl.ds(s * length, length), cols] for s in range(seqs)]

    def scores(p, carry):
        q = pair_cols(0, p)
        k = jnp.concatenate(pair_cols(1, p), axis=1)
        for half, mask in ((0, low), (1, high)):
            part = dot_t(jnp.concatenate([x * mask for x in q], axis=1), k)
            part = part.astype(BF).reshape(chips, 2, share, length)
            for c in range(2):
                sbuf[c, :, 2 * p + half] = part[:, c]
        return carry

    lax.fori_loop(0, heads // 2, scores, 0)
    pl.semaphore_wait(barrier, n - 1)

    swap = pltpu.make_async_remote_copy(
        src_ref=sbuf.at[1 - core], dst_ref=rbuf, send_sem=pair_sems.at[0], recv_sem=pair_sems.at[1],
        device_id={"depth": sibling}, device_id_type=MESH,
    )
    swap.start()
    swap.wait()

    def rs_copy(k):
        other = lax.rem(chip + k, chips)
        return pltpu.make_async_remote_copy(
            src_ref=tbuf.at[other], dst_ref=gbuf.at[k], send_sem=rs_send.at[k], recv_sem=rs_recv.at[k],
            device_id={"depth": other * 2 + core}, device_id_type=MESH,
        )

    def rs_start(k, carry):
        other = lax.rem(chip + k, chips)
        tbuf[other] = (sbuf[core, other].astype(F32) + rbuf[other].astype(F32)).astype(BF)
        rs_copy(k).start()
        return carry

    lax.fori_loop(1, chips, rs_start, 0)
    total = sbuf[core, chip].astype(F32) + rbuf[chip].astype(F32)

    def rs_add(k, total):
        rs_copy(k).wait_recv()
        return total + gbuf[k].astype(F32)

    total = lax.fori_loop(1, chips, rs_add, total)
    factor = 1.0 / (math.sqrt(head_size) * math.sqrt(seqs * n))
    mine = chain_col[pl.ds(pl.multiple_of(me * share, share), share), :]
    same = mine == chain_row[...]
    for h in range(heads):
        tied = total[h] * factor + jnp.where(same, bias_ref[1, h], bias_ref[0, h])
        top = jnp.max(tied, axis=-1, keepdims=True)
        weights = jnp.exp(tied - top)
        pbuf[me, h] = (weights / jnp.sum(weights, axis=-1, keepdims=True)).astype(BF)

    def ag_copy(k):
        other = lax.rem(chip + k, chips)
        return pltpu.make_async_remote_copy(
            src_ref=pbuf.at[me], dst_ref=pbuf.at[me], send_sem=ag_send.at[k], recv_sem=ag_recv.at[k],
            device_id={"depth": other * 2 + core}, device_id_type=MESH,
        )

    def fw_copy(k):
        origin = lax.rem(chip - k + chips, chips) * 2 + core
        return pltpu.make_async_remote_copy(
            src_ref=pbuf.at[origin], dst_ref=pbuf.at[origin], send_sem=fw_send.at[k], recv_sem=fw_recv.at[k],
            device_id={"depth": sibling}, device_id_type=MESH,
        )

    def ag_start(k, carry):
        ag_copy(k).start()
        return carry

    lax.fori_loop(1, chips, ag_start, 0)
    fw_copy(0).start()

    def ag_forward(k, carry):
        ag_copy(k).wait_recv()
        fw_copy(k).start()
        return carry

    lax.fori_loop(1, chips, ag_forward, 0)

    def fw_wait(k, carry):
        fw_copy(k).wait_recv()
        return carry

    lax.fori_loop(0, chips, fw_wait, 0)

    def mixing(p, carry):
        v = jnp.concatenate(pair_cols(2, p), axis=1)
        lows = jnp.concatenate([low] * seqs, axis=1)
        highs = jnp.concatenate([high] * seqs, axis=1)
        keys = jnp.concatenate([v * lows, v * highs], axis=0)
        probs = jnp.concatenate(
            [pbuf[:, 2 * p].reshape(length, length), pbuf[:, 2 * p + 1].reshape(length, length)], axis=1
        )
        mixed = dot(probs, keys).astype(BF)
        pair = 2 * head_size
        cols = pl.ds(pl.multiple_of(p * pair, pair), pair)
        for s in range(seqs):
            mix_ref[pl.ds(s * length, length), cols] = mixed[:, s * pair : (s + 1) * pair]
        return carry

    lax.fori_loop(0, heads // 2, mixing, 0)

    def finish(t, carry):
        cols = pl.ds(pl.multiple_of(t * 256, 256), 256)
        x1 = (x0_ref[:, cols] + dot(mix_ref[...], wo_ref[:, cols])).astype(BF)
        for s in range(seqs):
            xbuf[:, s, :, cols] = x1[s * length : (s + 1) * length].reshape(n, share, 256)
        return carry

    lax.fori_loop(0, width // 256, finish, 0)

    def aa_copy(k):
        other = lax.rem(me + k, n)
        return pltpu.make_async_remote_copy(
            src_ref=xbuf.at[other], dst_ref=out_ref.at[me], send_sem=aa_send.at[k], recv_sem=aa_recv.at[k],
            device_id={"depth": other}, device_id_type=MESH,
        )

    def aa_start(k, carry):
        aa_copy(k).start()
        return carry

    lax.fori_loop(1, n, aa_start, 0)
    keep = pltpu.make_async_copy(xbuf.at[me], out_ref.at[me], local_sem)
    keep.start()
    keep.wait()

    def drain(k, carry):
        aa_copy(k).wait()
        return carry

    lax.fori_loop(1, n, drain, 0)

    def drain_sends(k, carry):
        rs_copy(k).wait_send()
        ag_copy(k).wait_send()
        fw_copy(k).wait_send()
        return carry

    lax.fori_loop(1, chips, drain_sends, 0)
    fw_copy(0).wait_send()


def column_order(rows, all_seqs, cols, inverse):
    r = lax.broadcasted_iota(jnp.int32, (rows, rows), 0)
    c = lax.broadcasted_iota(jnp.int32, (rows, rows), 1)
    if inverse:
        r, c = c, r
    return jnp.where(c == (r % all_seqs) * cols + r // all_seqs, 1.0, 0.0).astype(BF)


def column_kernel(
    all_seqs, heads, head_size, x_ref, wqkv_ref, wo_ref, x2_ref, u3_ref, flat_ref, qkv_ref, mix_ref
):
    rows, width = x_ref.shape
    cols = rows // all_seqs
    flat_ref[...] = dot(column_order(rows, all_seqs, cols, False), x_ref[...])
    u2 = layer_norm(flat_ref[...]).astype(BF)
    project_into(u2, wqkv_ref, qkv_ref, 256)
    pair = 2 * head_size
    low, high = half_masks(pair)
    group = 128
    r = lax.broadcasted_iota(jnp.int32, (2 * group, group), 0)
    c = lax.broadcasted_iota(jnp.int32, (2 * group, group), 1)
    inside = (r % group) // all_seqs == c // all_seqs
    factor = 1.0 / math.sqrt(head_size)

    def attend(g, carry):
        here = pl.ds(pl.multiple_of(g * group, group), group)
        for p in range(heads // 2):
            q = qkv_ref[here, p * pair : (p + 1) * pair]
            k = qkv_ref[here, width + p * pair : width + (p + 1) * pair]
            v = qkv_ref[here, 2 * width + p * pair : 2 * width + (p + 1) * pair]
            scores = dot_t(jnp.concatenate([q * low, q * high], axis=0), k) * factor
            scores = jnp.where(inside, scores, -jnp.inf)
            top = jnp.max(scores, axis=-1, keepdims=True)
            weights = jnp.exp(scores - top)
            probs = (weights / jnp.sum(weights, axis=-1, keepdims=True)).astype(BF)
            probs = jnp.concatenate([probs[:group], probs[group:]], axis=1)
            values = jnp.concatenate([v * low, v * high], axis=0)
            mix_ref[here, p * pair : (p + 1) * pair] = dot(probs, values).astype(BF)
        return carry

    lax.fori_loop(0, rows // group, attend, 0)
    x2_ref[...] = flat_ref[...] + dot(mix_ref[...], wo_ref[...])
    u3_ref[...] = layer_norm(x2_ref[...]).astype(BF)


def feed_kernel(all_seqs, x2_ref, u3_ref, up_ref, down_ref, out_ref, acc_ref):
    rows = x2_ref.shape[0]
    acc_ref[...] = x2_ref[...]
    step = 512

    def body(t, carry):
        part = pl.ds(pl.multiple_of(t * step, step), step)
        pre = dot(u3_ref[...], up_ref[:, part])
        hidden = (0.5 * pre * (1.0 + lax.erf(pre * math.sqrt(0.5)))).astype(BF)
        acc_ref[...] += dot(hidden, down_ref[part, :])
        return carry

    lax.fori_loop(0, up_ref.shape[1] // step, body, 0)
    order = column_order(rows, all_seqs, rows // all_seqs, True)
    out_ref[...] = dot(order, acc_ref[...].astype(BF)).astype(BF)


def vmem_specs(count):
    return [pl.BlockSpec(memory_space=pltpu.VMEM)] * count


def fast_device(
    alignment_token_grid,
    residue_chain_index,
    alignment_state,
    embedding,
    chain_head_bias,
    row_query_key_value,
    row_output_weight,
    column_query_key_value,
    column_output_weight,
    feed_up_weight,
    feed_down_weight,
):
    seqs, length, width = alignment_state.shape
    heads = chain_head_bias.shape[1]
    head_size = width // heads
    n = lax.axis_size("depth")
    share = length // n
    rows = seqs * length
    all_seqs = seqs * n
    full_up = lax.all_gather(feed_up_weight, "depth", axis=0, tiled=True)
    full_down = lax.all_gather(feed_down_weight, "depth", axis=0, tiled=True)
    chunk = (heads, share, length)
    DMA = pltpu.SemaphoreType.DMA
    block = pl.pallas_call(
        functools.partial(row_kernel, n, seqs, length, heads, head_size),
        out_shape=jax.ShapeDtypeStruct((n, seqs, share, width), BF),
        in_specs=vmem_specs(5) + [pl.BlockSpec(memory_space=pltpu.SMEM)] + vmem_specs(2),
        out_specs=pl.BlockSpec(memory_space=pltpu.VMEM),
        scratch_shapes=[
            pltpu.VMEM((rows, width), F32),
            pltpu.VMEM((rows, 3 * width), BF),
            pltpu.VMEM((2, n // 2) + chunk, BF),
            pltpu.VMEM((n // 2,) + chunk, BF),
            pltpu.VMEM((n // 2,) + chunk, BF),
            pltpu.VMEM((n // 2,) + chunk, BF),
            pltpu.VMEM((n,) + chunk, BF),
            pltpu.VMEM((rows, width), BF),
            pltpu.VMEM((n, seqs, share, width), BF),
            DMA((2,)),
            DMA((n // 2,)), DMA((n // 2,)), DMA((n // 2,)), DMA((n // 2,)),
            DMA((n // 2,)), DMA((n // 2,)), DMA((n,)), DMA((n,)), DMA,
        ],
        compiler_params=pltpu.CompilerParams(
            collective_id=0, has_side_effects=True, vmem_limit_bytes=40 * 2**20
        ),
        cost_estimate=pl.CostEstimate(
            flops=2 * rows * width * width * 5, bytes_accessed=200 * 2**20, transcendentals=0
        ),
        name="row_stage",
    )(
        alignment_token_grid.reshape(rows, 1),
        residue_chain_index.reshape(length, 1),
        residue_chain_index.reshape(1, length),
        alignment_state.reshape(rows, width),
        embedding,
        chain_head_bias,
        row_query_key_value,
        row_output_weight,
    )
    x2, u3 = pl.pallas_call(
        functools.partial(column_kernel, all_seqs, heads, head_size),
        out_shape=(jax.ShapeDtypeStruct((rows, width), F32), jax.ShapeDtypeStruct((rows, width), BF)),
        in_specs=vmem_specs(3),
        out_specs=(pl.BlockSpec(memory_space=pltpu.VMEM),) * 2,
        scratch_shapes=[
            pltpu.VMEM((rows, width), F32),
            pltpu.VMEM((rows, 3 * width), BF),
            pltpu.VMEM((rows, width), BF),
        ],
        compiler_params=pltpu.CompilerParams(vmem_limit_bytes=40 * 2**20),
        cost_estimate=pl.CostEstimate(
            flops=2 * rows * width * width * 5, bytes_accessed=60 * 2**20, transcendentals=0
        ),
        name="column_stage",
    )(block.reshape(rows, width), column_query_key_value, column_output_weight)
    result = pl.pallas_call(
        functools.partial(feed_kernel, all_seqs),
        out_shape=jax.ShapeDtypeStruct((rows, width), BF),
        in_specs=vmem_specs(4),
        out_specs=pl.BlockSpec(memory_space=pltpu.VMEM),
        scratch_shapes=[pltpu.VMEM((rows, width), F32)],
        compiler_params=pltpu.CompilerParams(vmem_limit_bytes=48 * 2**20),
        cost_estimate=pl.CostEstimate(
            flops=2 * rows * width * width * 8, bytes_accessed=40 * 2**20, transcendentals=0
        ),
        name="feed_stage",
    )(x2, u3, full_up, full_down)
    return result.reshape(all_seqs, share, width)


def layer_norm(values):
    center = values - jnp.mean(values, axis=-1, keepdims=True)
    spread = jnp.mean(center * center, axis=-1, keepdims=True)
    return center * lax.rsqrt(spread + 1e-05)


def chain_terms(query_ids, residue_chain_index, chain_head_bias):
    same = query_ids[:, None] == residue_chain_index[None, :]
    return jnp.where(
        same[:, None, :], chain_head_bias[1][None, :, None], chain_head_bias[0][None, :, None]
    )


def plain_device(
    alignment_token_grid,
    residue_chain_index,
    alignment_state,
    embedding,
    chain_head_bias,
    row_query_key_value,
    row_output_weight,
    column_query_key_value,
    column_output_weight,
    feed_up_weight,
    feed_down_weight,
):
    device_sequences = alignment_state.shape[0]
    residue_length = alignment_state.shape[1]
    hidden_width = alignment_state.shape[2]
    heads = chain_head_bias.shape[1]
    head_size = hidden_width // heads
    devices = lax.axis_size("depth")
    all_seqs = device_sequences * devices
    token_letters = embedding.shape[0]
    one_hot = (
        alignment_token_grid.reshape(-1)[:, None]
        == jnp.arange(token_letters, dtype=jnp.int32)[None, :]
    ).astype(jnp.bfloat16)
    initial_input0 = alignment_state.reshape(-1, hidden_width).astype(jnp.float32) + jnp.dot(
        one_hot, embedding, preferred_element_type=jnp.float32
    )
    u1 = layer_norm(initial_input0).astype(jnp.bfloat16)
    qkv1 = jnp.dot(u1, row_query_key_value, preferred_element_type=jnp.float32).astype(jnp.bfloat16)
    qkv1 = qkv1.reshape(device_sequences, residue_length, 3, heads, head_size)
    queries = qkv1[:, :, 0]
    keys_row = qkv1[:, :, 1]
    values_row = qkv1[:, :, 2]
    factor = 1.0 / (math.sqrt(head_size) * math.sqrt(all_seqs))
    partial_value = jnp.einsum(
        "sihd,sjhd->ihj", queries, keys_row, preferred_element_type=jnp.float32
    )
    tied = lax.psum(partial_value, "depth") * factor
    tied = tied + chain_terms(residue_chain_index, residue_chain_index, chain_head_bias)
    row_probs = jax.nn.softmax(tied, axis=-1).astype(jnp.bfloat16)
    row_mix = jnp.einsum(
        "ihj,sjhd->sihd", row_probs, values_row, preferred_element_type=jnp.float32
    ).astype(jnp.bfloat16)
    x1 = initial_input0 + jnp.dot(
        row_mix.reshape(-1, hidden_width), row_output_weight, preferred_element_type=jnp.float32
    )
    col_share = residue_length // devices
    x1 = x1.astype(jnp.bfloat16).reshape(device_sequences, devices, col_share, hidden_width)
    block = lax.all_to_all(x1, "depth", split_axis=1, concat_axis=0, tiled=True)
    seqs_here = block.shape[0]
    cols = block.shape[2]
    flat = block.reshape(seqs_here * cols, hidden_width).astype(jnp.float32)
    u2 = layer_norm(flat).astype(jnp.bfloat16)
    qkv2 = jnp.dot(u2, column_query_key_value, preferred_element_type=jnp.float32).astype(
        jnp.bfloat16
    )
    qkv2 = qkv2.reshape(seqs_here, cols, 3, heads, head_size)
    scores = jnp.einsum(
        "snhd,tnhd->nhst", qkv2[:, :, 0], qkv2[:, :, 1], preferred_element_type=jnp.float32
    ) / math.sqrt(head_size)
    col_probs = jax.nn.softmax(scores, axis=-1).astype(jnp.bfloat16)
    col_mix = jnp.einsum(
        "nhst,tnhd->snhd", col_probs, qkv2[:, :, 2], preferred_element_type=jnp.float32
    ).astype(jnp.bfloat16)
    result = flat + jnp.dot(
        col_mix.reshape(seqs_here * cols, hidden_width),
        column_output_weight,
        preferred_element_type=jnp.float32,
    )
    x2 = result.reshape(seqs_here, 1, cols, hidden_width)
    out_shape = (x2.shape[0], x2.shape[2], hidden_width)
    flat2 = x2.reshape(-1, hidden_width)
    u3 = layer_norm(flat2).astype(jnp.bfloat16)
    full_up, full_down = (
        lax.all_gather(feed_up_weight, "depth", axis=0, tiled=True),
        lax.all_gather(feed_down_weight, "depth", axis=0, tiled=True),
    )
    pre = jnp.dot(u3, full_up, preferred_element_type=jnp.float32)
    hidden = jax.nn.gelu(pre, approximate=False).astype(jnp.bfloat16)
    projected = jnp.dot(hidden, full_down, preferred_element_type=jnp.float32)
    return (flat2 + projected).astype(jnp.bfloat16).reshape(out_shape)


def per_device(*arrays):
    seqs, length, width = arrays[2].shape
    heads = arrays[4].shape[1]
    n = lax.axis_size("depth")
    fits = (
        n % 2 == 0
        and length % n == 0
        and (length // n) % 16 == 0
        and 128 % (seqs * n) == 0
        and (seqs * length) % 128 == 0
        and 2 * (width // heads) == 128
        and heads % 2 == 0
        and width % 256 == 0
    )
    return (fast_device if fits else plain_device)(*arrays)


def solution(mesh):
    in_specs = (
        P(("groups", "depth"), None),
        P("groups"),
        P(("groups", "depth"), None, None),
        P(),
        P(),
        P(),
        P(),
        P(),
        P(),
        P("depth", None),
        P("depth", None),
    )
    out_specs = P("groups", "depth", None)
    return jax.shard_map(
        per_device, mesh=mesh, in_specs=in_specs, out_specs=out_specs, check_vma=False
    )
```

```python
import functools
import math

import jax
import jax.numpy as jnp
from jax import lax
from jax.experimental import pallas as pl
from jax.experimental.pallas import tpu as pltpu
from jax.sharding import PartitionSpec as P

MESH = pl.DeviceIdType.MESH
BF = jnp.bfloat16
F32 = jnp.float32


def dot(a, b):
    return jnp.dot(a, b, preferred_element_type=F32)


def dot_t(a, b):
    return lax.dot_general(a, b, (((1,), (1,)), ((), ())), preferred_element_type=F32)


def half_masks(width):
    lane = lax.broadcasted_iota(jnp.int32, (1, width), 1)
    low = jnp.where(lane < width // 2, 1.0, 0.0)
    return low.astype(BF), (1.0 - low).astype(BF)


def project_into(source, weight_ref, target_ref, step):
    def body(t, carry):
        cols = pl.ds(pl.multiple_of(t * step, step), step)
        target_ref[:, cols] = dot(source, weight_ref[:, cols]).astype(BF)
        return carry

    lax.fori_loop(0, weight_ref.shape[1] // step, body, 0)


def layer_kernel(
    n, seqs, length, heads, head_size,
    tok_any, chain_any, state_any, emb_any, bias_any, wqkv_any, wo_any, wqkv2_any, wo2_any, up_any, down_any,
    out_ref,
    tok_ref, chain_row, state_ref, emb_ref, bias_ref, wqkv_ref, wo_ref, wqkv2_ref, wo2_ref, up_ref, down_ref,
    x0_ref, qkv_ref, sbuf, rbuf, tbuf, gbuf, pbuf, mix_ref, xbuf, block_ref,
    load_sems, pair_sems, rs_send, rs_recv, ag_send, ag_recv, fw_send, fw_recv, aa_send, aa_recv, local_sem,
    z_send, z_recv, y_send, y_recv, c_send, c_recv,
):
    me = lax.axis_index("depth")
    core = lax.rem(me, 2)
    chip = me // 2
    chips = n // 2
    sibling = me + 1 - 2 * core
    share = length // n
    width = heads * head_size
    z_size = n // 4
    my_y = lax.rem(chip, 2)
    my_z = chip // 2

    loads = [
        pltpu.make_async_copy(source, target, load_sems.at[k])
        for k, (source, target) in enumerate(
            (
                (up_any, up_ref.at[me]),
                (down_any, down_ref.at[me]),
                (tok_any, tok_ref),
                (emb_any, emb_ref),
                (state_any, state_ref),
                (chain_any, chain_row),
                (bias_any, bias_ref),
                (wqkv_any, wqkv_ref),
                (wo_any, wo_ref),
                (wqkv2_any, wqkv2_ref),
                (wo2_any, wo2_ref),
            )
        )
    ]
    for load in loads:
        load.start()

    barrier = pltpu.get_barrier_semaphore()

    def greet(k, carry):
        pl.semaphore_signal(
            barrier, inc=1, device_id={"depth": lax.rem(me + k, n)}, device_id_type=MESH
        )
        return carry

    lax.fori_loop(1, n, greet, 0)

    def place(z, y, c):
        return (z * 2 + y) * 2 + c

    def hop(index, target, send, recv, at):
        return [
            pltpu.make_async_remote_copy(
                src_ref=ref.at[index], dst_ref=ref.at[index],
                send_sem=send.at[(w,) + at], recv_sem=recv.at[(w,) + at],
                device_id={"depth": target}, device_id_type=MESH,
            )
            for w, ref in ((0, up_ref), (1, down_ref))
        ]

    def z_hop(step, sign, origin, target):
        return hop(place(origin, my_y, core), place(target, my_y, core), z_send, z_recv, (0 if sign > 0 else 1, step))

    def y_hop(origin, y):
        return hop(place(origin, y, core), place(my_z, 1 - my_y, core), y_send, y_recv, (origin,))

    def c_hop(origin, y, c):
        return hop(place(origin, y, c), sibling, c_send, c_recv, (origin, y))

    def start(copies):
        for copy in copies:
            copy.start()

    def wait_recv(copies):
        for copy in copies:
            copy.wait_recv()

    def wait_send(copies):
        for copy in copies:
            copy.wait_send()

    def on_line(z):
        return jnp.logical_and(z >= 0, z < z_size)

    def weights_first():
        for sign in (1, -1):

            @pl.when(on_line(my_z + sign))
            def _():
                start(z_hop(1, sign, my_z, my_z + sign))

        start(y_hop(my_z, my_y))
        start(c_hop(my_z, my_y, core))

    def weights_step(step):
        for sign in (1, -1):
            origin = my_z - sign * step

            @pl.when(on_line(origin))
            def _():
                wait_recv(z_hop(step, sign, origin, my_z))

                @pl.when(on_line(my_z + sign))
                def _():
                    start(z_hop(step + 1, sign, origin, my_z + sign))

                start(y_hop(origin, my_y))
                start(c_hop(origin, my_y, core))

    def weights_across(k):
        origin = lax.rem(my_z + k, z_size)
        wait_recv(y_hop(origin, 1 - my_y))
        start(c_hop(origin, 1 - my_y, core))

    def weights_ready():
        for origin in range(z_size):
            for y in range(2):
                wait_recv(c_hop(origin, y, 1 - core))

    def weights_drain():
        for sign in (1, -1):
            for step in range(1, z_size):
                origin = my_z - sign * (step - 1)

                @pl.when(jnp.logical_and(on_line(origin), on_line(my_z + sign)))
                def _():
                    wait_send(z_hop(step, sign, origin, my_z + sign))

        for origin in range(z_size):
            wait_send(y_hop(origin, my_y))
            for y in range(2):
                wait_send(c_hop(origin, y, core))

    for load in loads[:5]:
        load.wait()
    pl.semaphore_wait(barrier, n - 1)
    weights_first()

    letters = lax.broadcasted_iota(jnp.int32, (emb_ref.shape[0], length), 0)
    for s in range(seqs):
        one_hot = jnp.where(tok_ref[s : s + 1, :] == letters, 1.0, 0.0).astype(BF)
        picked = lax.dot_general(one_hot, emb_ref[...], (((0,), (0,)), ((), ())), preferred_element_type=F32)
        x0_ref[s * length : (s + 1) * length, :] = (
            state_ref[s * length : (s + 1) * length, :].astype(F32) + picked
        )
    u1 = layer_norm(x0_ref[...]).astype(BF)
    for load in loads[5:]:
        load.wait()
    project_into(u1, wqkv_ref, qkv_ref, 256)
    low, high = half_masks(2 * head_size)

    def pair_cols(which, p):
        cols = pl.ds(pl.multiple_of(which * width + p * 2 * head_size, 2 * head_size), 2 * head_size)
        return [qkv_ref[pl.ds(s * length, length), cols] for s in range(seqs)]

    def scores(p, carry):
        q = pair_cols(0, p)
        k = jnp.concatenate(pair_cols(1, p), axis=1)
        for half, mask in ((0, low), (1, high)):
            part = dot_t(jnp.concatenate([x * mask for x in q], axis=1), k)
            part = part.astype(BF).reshape(chips, 2, share, length)
            for c in range(2):
                sbuf[c, :, 2 * p + half] = part[:, c]
        return carry

    lax.fori_loop(0, heads // 2, scores, 0)

    swap = pltpu.make_async_remote_copy(
        src_ref=sbuf.at[1 - core], dst_ref=rbuf, send_sem=pair_sems.at[0], recv_sem=pair_sems.at[1],
        device_id={"depth": sibling}, device_id_type=MESH,
    )
    swap.start()
    weights_step(1)
    swap.wait()

    def rs_copy(k):
        other = lax.rem(chip + k, chips)
        return pltpu.make_async_remote_copy(
            src_ref=tbuf.at[other], dst_ref=gbuf.at[k], send_sem=rs_send.at[k], recv_sem=rs_recv.at[k],
            device_id={"depth": other * 2 + core}, device_id_type=MESH,
        )

    def rs_start(k, carry):
        other = lax.rem(chip + k, chips)
        tbuf[other] = (sbuf[core, other].astype(F32) + rbuf[other].astype(F32)).astype(BF)
        rs_copy(k).start()
        return carry

    lax.fori_loop(1, chips, rs_start, 0)
    weights_across(0)
    total = sbuf[core, chip].astype(F32) + rbuf[chip].astype(F32)

    def rs_add(k, total):
        rs_copy(k).wait_recv()
        return total + gbuf[k].astype(F32)

    total = lax.fori_loop(1, chips, rs_add, total)
    factor = 1.0 / (math.sqrt(head_size) * math.sqrt(seqs * n))
    spot = lax.broadcasted_iota(jnp.int32, (share, length), 1)
    row = lax.broadcasted_iota(jnp.int32, (share, length), 0) + me * share
    mine = jnp.sum(jnp.where(spot == row, chain_row[...], 0), axis=-1, keepdims=True)
    same = mine == chain_row[...]
    for h in range(heads):
        tied = total[h] * factor + jnp.where(same, bias_ref[1:2, h : h + 1], bias_ref[0:1, h : h + 1])
        top = jnp.max(tied, axis=-1, keepdims=True)
        weights = jnp.exp(tied - top)
        pbuf[me, h] = (weights / jnp.sum(weights, axis=-1, keepdims=True)).astype(BF)

    def ag_copy(k):
        other = lax.rem(chip + k, chips)
        return pltpu.make_async_remote_copy(
            src_ref=pbuf.at[me], dst_ref=pbuf.at[me], send_sem=ag_send.at[k], recv_sem=ag_recv.at[k],
            device_id={"depth": other * 2 + core}, device_id_type=MESH,
        )

    def fw_copy(k):
        origin = lax.rem(chip - k + chips, chips) * 2 + core
        return pltpu.make_async_remote_copy(
            src_ref=pbuf.at[origin], dst_ref=pbuf.at[origin], send_sem=fw_send.at[k], recv_sem=fw_recv.at[k],
            device_id={"depth": sibling}, device_id_type=MESH,
        )

    def ag_start(k, carry):
        ag_copy(k).start()
        return carry

    lax.fori_loop(1, chips, ag_start, 0)
    fw_copy(0).start()
    for step in range(2, 3):
        weights_step(step)

    def ag_forward(k, carry):
        ag_copy(k).wait_recv()
        fw_copy(k).start()
        return carry

    lax.fori_loop(1, chips, ag_forward, 0)

    def fw_wait(k, carry):
        fw_copy(k).wait_recv()
        return carry

    lax.fori_loop(0, chips, fw_wait, 0)
    for step in range(3, z_size):
        weights_step(step)

    def mixing(p, carry):
        v = jnp.concatenate(pair_cols(2, p), axis=1)
        lows = jnp.concatenate([low] * seqs, axis=1)
        highs = jnp.concatenate([high] * seqs, axis=1)
        keys = jnp.concatenate([v * lows, v * highs], axis=0)
        probs = jnp.concatenate(
            [pbuf[:, 2 * p].reshape(length, length), pbuf[:, 2 * p + 1].reshape(length, length)], axis=1
        )
        mixed = dot(probs, keys).astype(BF)
        pair = 2 * head_size
        cols = pl.ds(pl.multiple_of(p * pair, pair), pair)
        for s in range(seqs):
            mix_ref[pl.ds(s * length, length), cols] = mixed[:, s * pair : (s + 1) * pair]
        return carry

    lax.fori_loop(0, heads // 2, mixing, 0)

    def finish(t, carry):
        cols = pl.ds(pl.multiple_of(t * 256, 256), 256)
        x1 = (x0_ref[:, cols] + dot(mix_ref[...], wo_ref[:, cols])).astype(BF)
        for s in range(seqs):
            xbuf[:, s, :, cols] = x1[s * length : (s + 1) * length].reshape(n, share, 256)
        return carry

    lax.fori_loop(0, width // 256, finish, 0)

    def aa_copy(k):
        other = lax.rem(me + k, n)
        return pltpu.make_async_remote_copy(
            src_ref=xbuf.at[other], dst_ref=block_ref.at[me], send_sem=aa_send.at[k], recv_sem=aa_recv.at[k],
            device_id={"depth": other}, device_id_type=MESH,
        )

    def aa_start(k, carry):
        aa_copy(k).start()
        return carry

    lax.fori_loop(1, n, aa_start, 0)
    keep = pltpu.make_async_copy(xbuf.at[me], block_ref.at[me], local_sem)
    keep.start()
    keep.wait()
    for k in range(1, z_size):
        weights_across(k)

    def drain(k, carry):
        aa_copy(k).wait()
        return carry

    lax.fori_loop(1, n, drain, 0)

    def drain_sends(k, carry):
        rs_copy(k).wait_send()
        ag_copy(k).wait_send()
        fw_copy(k).wait_send()
        return carry

    lax.fori_loop(1, chips, drain_sends, 0)
    fw_copy(0).wait_send()

    rows = seqs * length
    all_seqs = seqs * n
    column_part(all_seqs, heads, head_size, block_ref, wqkv2_ref, wo2_ref, x0_ref, qkv_ref, mix_ref)
    weights_ready()
    u3 = layer_norm(x0_ref[...]).astype(BF)
    mix_ref[...] = u3
    feed_part(mix_ref, up_ref, down_ref, x0_ref)
    order = column_order(rows, all_seqs, share, True)
    out_ref[...] = dot(order, x0_ref[...].astype(BF)).astype(BF)
    weights_drain()


def column_order(rows, all_seqs, cols, inverse):
    r = lax.broadcasted_iota(jnp.int32, (rows, rows), 0)
    c = lax.broadcasted_iota(jnp.int32, (rows, rows), 1)
    if inverse:
        r, c = c, r
    return jnp.where(c == (r % all_seqs) * cols + r // all_seqs, 1.0, 0.0).astype(BF)


def column_part(all_seqs, heads, head_size, block_ref, wqkv_ref, wo_ref, flat_ref, qkv_ref, mix_ref):
    rows, width = flat_ref.shape
    cols = rows // all_seqs
    flat_ref[...] = dot(column_order(rows, all_seqs, cols, False), block_ref[...].reshape(rows, width))
    u2 = layer_norm(flat_ref[...]).astype(BF)
    project_into(u2, wqkv_ref, qkv_ref, 256)
    pair = 2 * head_size
    low, high = half_masks(pair)
    group = 128
    r = lax.broadcasted_iota(jnp.int32, (2 * group, group), 0)
    c = lax.broadcasted_iota(jnp.int32, (2 * group, group), 1)
    inside = (r % group) // all_seqs == c // all_seqs
    factor = 1.0 / math.sqrt(head_size)

    def attend(g, carry):
        here = pl.ds(pl.multiple_of(g * group, group), group)
        for p in range(heads // 2):
            q = qkv_ref[here, p * pair : (p + 1) * pair]
            k = qkv_ref[here, width + p * pair : width + (p + 1) * pair]
            v = qkv_ref[here, 2 * width + p * pair : 2 * width + (p + 1) * pair]
            scores = dot_t(jnp.concatenate([q * low, q * high], axis=0), k) * factor
            scores = jnp.where(inside, scores, -jnp.inf)
            top = jnp.max(scores, axis=-1, keepdims=True)
            weights = jnp.exp(scores - top)
            probs = (weights / jnp.sum(weights, axis=-1, keepdims=True)).astype(BF)
            probs = jnp.concatenate([probs[:group], probs[group:]], axis=1)
            values = jnp.concatenate([v * low, v * high], axis=0)
            mix_ref[here, p * pair : (p + 1) * pair] = dot(probs, values).astype(BF)
        return carry

    lax.fori_loop(0, rows // group, attend, 0)
    flat_ref[...] += dot(mix_ref[...], wo_ref[...])


def feed_part(u3_ref, up_ref, down_ref, acc_ref):
    n, up_rows, hidden_size = up_ref.shape
    down_rows, width = down_ref.shape[1:]
    span = max(d for d in range(1, n + 1) if n % d == 0 and d * down_rows <= 768)
    step = span * down_rows

    def body(t, carry):
        part = pl.ds(pl.multiple_of(t * step, step), step)
        pre = dot(u3_ref[...], up_ref[:, :, part].reshape(n * up_rows, step))
        hidden = (0.5 * pre * (1.0 + lax.erf(pre * math.sqrt(0.5)))).astype(BF)
        acc_ref[...] += dot(hidden, down_ref[pl.ds(t * span, span)].reshape(step, width))
        return carry

    lax.fori_loop(0, hidden_size // step, body, 0)


def fast_device(
    alignment_token_grid,
    residue_chain_index,
    alignment_state,
    embedding,
    chain_head_bias,
    row_query_key_value,
    row_output_weight,
    column_query_key_value,
    column_output_weight,
    feed_up_weight,
    feed_down_weight,
):
    seqs, length, width = alignment_state.shape
    heads = chain_head_bias.shape[1]
    head_size = width // heads
    n = lax.axis_size("depth")
    share = length // n
    rows = seqs * length
    all_seqs = seqs * n
    chunk = (heads, share, length)
    arrays = (
        alignment_token_grid,
        residue_chain_index.reshape(1, length),
        alignment_state.reshape(rows, width),
        embedding,
        chain_head_bias,
        row_query_key_value,
        row_output_weight,
        column_query_key_value,
        column_output_weight,
    )
    DMA = pltpu.SemaphoreType.DMA
    half = n // 2
    deep = n // 4
    result = pl.pallas_call(
        functools.partial(layer_kernel, n, seqs, length, heads, head_size),
        out_shape=jax.ShapeDtypeStruct((rows, width), BF),
        in_specs=[pl.BlockSpec(memory_space=pl.ANY)] * 11,
        out_specs=pl.BlockSpec(memory_space=pltpu.VMEM),
        scratch_shapes=[pltpu.VMEM(x.shape, x.dtype) for x in arrays]
        + [
            pltpu.VMEM((n,) + feed_up_weight.shape, BF),
            pltpu.VMEM((n,) + feed_down_weight.shape, BF),
            pltpu.VMEM((rows, width), F32),
            pltpu.VMEM((rows, 3 * width), BF),
            pltpu.VMEM((2, half) + chunk, BF),
            pltpu.VMEM((half,) + chunk, BF),
            pltpu.VMEM((half,) + chunk, BF),
            pltpu.VMEM((half,) + chunk, BF),
            pltpu.VMEM((n,) + chunk, BF),
            pltpu.VMEM((rows, width), BF),
            pltpu.VMEM((n, seqs, share, width), BF),
            pltpu.VMEM((n, seqs, share, width), BF),
            DMA((11,)), DMA((2,)),
            DMA((half,)), DMA((half,)), DMA((half,)), DMA((half,)),
            DMA((half,)), DMA((half,)), DMA((n,)), DMA((n,)), DMA,
            DMA((2, 2, deep)), DMA((2, 2, deep)), DMA((2, deep)), DMA((2, deep)),
            DMA((2, deep, 2)), DMA((2, deep, 2)),
        ],
        compiler_params=pltpu.CompilerParams(
            collective_id=0, has_side_effects=True, vmem_limit_bytes=58 * 2**20
        ),
        cost_estimate=pl.CostEstimate(
            flops=2 * rows * width * width * 18, bytes_accessed=40 * 2**20, transcendentals=0
        ),
        name="layer",
    )(*arrays, feed_up_weight, feed_down_weight)
    return result.reshape(all_seqs, share, width)


def layer_norm(values):
    center = values - jnp.mean(values, axis=-1, keepdims=True)
    spread = jnp.mean(center * center, axis=-1, keepdims=True)
    return center * lax.rsqrt(spread + 1e-05)


def chain_terms(query_ids, residue_chain_index, chain_head_bias):
    same = query_ids[:, None] == residue_chain_index[None, :]
    return jnp.where(
        same[:, None, :], chain_head_bias[1][None, :, None], chain_head_bias[0][None, :, None]
    )


def plain_device(
    alignment_token_grid,
    residue_chain_index,
    alignment_state,
    embedding,
    chain_head_bias,
    row_query_key_value,
    row_output_weight,
    column_query_key_value,
    column_output_weight,
    feed_up_weight,
    feed_down_weight,
):
    device_sequences = alignment_state.shape[0]
    residue_length = alignment_state.shape[1]
    hidden_width = alignment_state.shape[2]
    heads = chain_head_bias.shape[1]
    head_size = hidden_width // heads
    devices = lax.axis_size("depth")
    all_seqs = device_sequences * devices
    token_letters = embedding.shape[0]
    one_hot = (
        alignment_token_grid.reshape(-1)[:, None]
        == jnp.arange(token_letters, dtype=jnp.int32)[None, :]
    ).astype(jnp.bfloat16)
    initial_input0 = alignment_state.reshape(-1, hidden_width).astype(jnp.float32) + jnp.dot(
        one_hot, embedding, preferred_element_type=jnp.float32
    )
    u1 = layer_norm(initial_input0).astype(jnp.bfloat16)
    qkv1 = jnp.dot(u1, row_query_key_value, preferred_element_type=jnp.float32).astype(jnp.bfloat16)
    qkv1 = qkv1.reshape(device_sequences, residue_length, 3, heads, head_size)
    queries = qkv1[:, :, 0]
    keys_row = qkv1[:, :, 1]
    values_row = qkv1[:, :, 2]
    factor = 1.0 / (math.sqrt(head_size) * math.sqrt(all_seqs))
    partial_value = jnp.einsum(
        "sihd,sjhd->ihj", queries, keys_row, preferred_element_type=jnp.float32
    )
    tied = lax.psum(partial_value, "depth") * factor
    tied = tied + chain_terms(residue_chain_index, residue_chain_index, chain_head_bias)
    row_probs = jax.nn.softmax(tied, axis=-1).astype(jnp.bfloat16)
    row_mix = jnp.einsum(
        "ihj,sjhd->sihd", row_probs, values_row, preferred_element_type=jnp.float32
    ).astype(jnp.bfloat16)
    x1 = initial_input0 + jnp.dot(
        row_mix.reshape(-1, hidden_width), row_output_weight, preferred_element_type=jnp.float32
    )
    col_share = residue_length // devices
    x1 = x1.astype(jnp.bfloat16).reshape(device_sequences, devices, col_share, hidden_width)
    block = lax.all_to_all(x1, "depth", split_axis=1, concat_axis=0, tiled=True)
    seqs_here = block.shape[0]
    cols = block.shape[2]
    flat = block.reshape(seqs_here * cols, hidden_width).astype(jnp.float32)
    u2 = layer_norm(flat).astype(jnp.bfloat16)
    qkv2 = jnp.dot(u2, column_query_key_value, preferred_element_type=jnp.float32).astype(
        jnp.bfloat16
    )
    qkv2 = qkv2.reshape(seqs_here, cols, 3, heads, head_size)
    scores = jnp.einsum(
        "snhd,tnhd->nhst", qkv2[:, :, 0], qkv2[:, :, 1], preferred_element_type=jnp.float32
    ) / math.sqrt(head_size)
    col_probs = jax.nn.softmax(scores, axis=-1).astype(jnp.bfloat16)
    col_mix = jnp.einsum(
        "nhst,tnhd->snhd", col_probs, qkv2[:, :, 2], preferred_element_type=jnp.float32
    ).astype(jnp.bfloat16)
    result = flat + jnp.dot(
        col_mix.reshape(seqs_here * cols, hidden_width),
        column_output_weight,
        preferred_element_type=jnp.float32,
    )
    x2 = result.reshape(seqs_here, 1, cols, hidden_width)
    out_shape = (x2.shape[0], x2.shape[2], hidden_width)
    flat2 = x2.reshape(-1, hidden_width)
    u3 = layer_norm(flat2).astype(jnp.bfloat16)
    full_up, full_down = (
        lax.all_gather(feed_up_weight, "depth", axis=0, tiled=True),
        lax.all_gather(feed_down_weight, "depth", axis=0, tiled=True),
    )
    pre = jnp.dot(u3, full_up, preferred_element_type=jnp.float32)
    hidden = jax.nn.gelu(pre, approximate=False).astype(jnp.bfloat16)
    projected = jnp.dot(hidden, full_down, preferred_element_type=jnp.float32)
    return (flat2 + projected).astype(jnp.bfloat16).reshape(out_shape)


def per_device(*arrays):
    seqs, length, width = arrays[2].shape
    heads = arrays[4].shape[1]
    n = lax.axis_size("depth")
    fits = (
        n % 2 == 0
        and length % n == 0
        and (length // n) % 16 == 0
        and n % 4 == 0
        and arrays[9].shape[0] % 16 == 0
        and arrays[10].shape[0] % 64 == 0
        and 128 % (seqs * n) == 0
        and (seqs * length) % 128 == 0
        and 2 * (width // heads) == 128
        and heads % 2 == 0
        and width % 256 == 0
    )
    return (fast_device if fits else plain_device)(*arrays)


def solution(mesh):
    in_specs = (
        P(("groups", "depth"), None),
        P("groups"),
        P(("groups", "depth"), None, None),
        P(),
        P(),
        P(),
        P(),
        P(),
        P(),
        P("depth", None),
        P("depth", None),
    )
    out_specs = P("groups", "depth", None)
    return jax.shard_map(
        per_device, mesh=mesh, in_specs=in_specs, out_specs=out_specs, check_vma=False
    )
```

```python
import functools
import math

import jax
import jax.numpy as jnp
from jax import lax
from jax.experimental import pallas as pl
from jax.experimental.pallas import tpu as pltpu
from jax.sharding import PartitionSpec as P

MESH = pl.DeviceIdType.MESH
BF = jnp.bfloat16
F32 = jnp.float32


def dot(a, b):
    return jnp.dot(a, b, preferred_element_type=F32)


def dot_t(a, b):
    return lax.dot_general(a, b, (((1,), (1,)), ((), ())), preferred_element_type=F32)


def half_masks(width):
    lane = lax.broadcasted_iota(jnp.int32, (1, width), 1)
    low = jnp.where(lane < width // 2, 1.0, 0.0)
    return low.astype(BF), (1.0 - low).astype(BF)


def project_into(source, weight_ref, target_ref, step):
    def body(t, carry):
        cols = pl.ds(pl.multiple_of(t * step, step), step)
        target_ref[:, cols] = dot(source, weight_ref[:, cols]).astype(BF)
        return carry

    lax.fori_loop(0, weight_ref.shape[1] // step, body, 0)


def layer_kernel(
    n, seqs, length, heads, head_size,
    tok_any, chain_any, state_any, emb_any, bias_any, wqkv_any, wo_any, wqkv2_any, wo2_any, up_any, down_any,
    out_ref,
    tok_ref, chain_row, state_ref, emb_ref, bias_ref, wqkv_ref, wo_ref, wqkv2_ref, wo2_ref, up_ref, down_ref,
    x0_ref, qkv_ref, sbuf, rbuf, tbuf, gbuf, pbuf, mix_ref, xbuf, block_ref,
    load_sems, pair_sems, rs_send, rs_recv, ag_send, ag_recv, fw_send, fw_recv, aa_send, aa_recv, local_sem,
    z_send, z_recv, y_send, y_recv, c_send, c_recv, x_send, x_recv,
):
    me = lax.axis_index("depth")
    core = lax.rem(me, 2)
    chip = me // 2
    chips = n // 2
    sibling = me + 1 - 2 * core
    share = length // n
    width = heads * head_size
    z_size = n // 4
    my_y = lax.rem(chip, 2)
    my_z = chip // 2
    group = lax.axis_index("groups")

    loads = [
        pltpu.make_async_copy(source, target, load_sems.at[k])
        for k, (source, target) in enumerate(
            (
                (up_any, up_ref.at[me]),
                (down_any, down_ref.at[me]),
                (tok_any, tok_ref),
                (emb_any, emb_ref),
                (state_any, state_ref),
                (chain_any, chain_row),
                (bias_any, bias_ref),
                (wqkv_any, wqkv_ref),
                (wo_any, wo_ref),
                (wqkv2_any, wqkv2_ref),
                (wo2_any, wo2_ref),
            )
        )
    ]
    for load in loads:
        load.start()

    barrier = pltpu.get_barrier_semaphore()

    def greet(k, carry):
        pl.semaphore_signal(
            barrier, inc=1, device_id={"depth": lax.rem(me + k, n)}, device_id_type=MESH
        )
        return carry

    lax.fori_loop(1, n, greet, 0)
    pl.semaphore_signal(barrier, inc=1, device_id={"groups": 1 - group}, device_id_type=MESH)

    def place(z, y, c):
        return (z * 2 + y) * 2 + c

    def hop(index, target, send, recv, at):
        return [
            pltpu.make_async_remote_copy(
                src_ref=ref.at[index], dst_ref=ref.at[index],
                send_sem=send.at[(w,) + at], recv_sem=recv.at[(w,) + at],
                device_id=target if isinstance(target, dict) else {"depth": target},
                device_id_type=MESH,
            )
            for w, ref in ((0, up_ref), (1, down_ref))
        ]

    def z_hop(step, sign, origin, target):
        return hop(place(origin, my_y, core), place(target, my_y, core), z_send, z_recv, (0 if sign > 0 else 1, step))

    def y_hop(origin, y):
        return hop(place(origin, y, core), place(my_z, 1 - my_y, core), y_send, y_recv, (origin,))

    def c_hop(origin, y, c):
        return hop(place(origin, y, c), sibling, c_send, c_recv, (origin, y))

    def x_hop(origin, y):
        return hop(place(origin, y, core), {"groups": 1 - group}, x_send, x_recv, (origin, y))

    def start(copies, mine=True):
        for w, copy in enumerate(copies):
            pl.when(group == (w if mine else 1 - w))(copy.start)

    def wait_recv(copies, mine=True):
        for w, copy in enumerate(copies):
            pl.when(group == (w if mine else 1 - w))(copy.wait_recv)

    def wait_send(copies, mine=True):
        for w, copy in enumerate(copies):
            pl.when(group == (w if mine else 1 - w))(copy.wait_send)

    def on_line(z):
        return jnp.logical_and(z >= 0, z < z_size)

    def weights_first():
        for sign in (1, -1):

            @pl.when(on_line(my_z + sign))
            def _():
                start(z_hop(1, sign, my_z, my_z + sign))

        start(y_hop(my_z, my_y))
        start(c_hop(my_z, my_y, core))
        start(c_hop(my_z, my_y, core), False)

    def weights_step(step):
        for sign in (1, -1):
            origin = my_z - sign * step

            @pl.when(on_line(origin))
            def _():
                wait_recv(z_hop(step, sign, origin, my_z))

                @pl.when(on_line(my_z + sign))
                def _():
                    start(z_hop(step + 1, sign, origin, my_z + sign))

                start(y_hop(origin, my_y))
                start(x_hop(origin, my_y))
                start(c_hop(origin, my_y, core))

    def weights_across(k):
        origin = lax.rem(my_z + k, z_size)
        wait_recv(y_hop(origin, 1 - my_y))
        start(x_hop(origin, 1 - my_y))
        start(c_hop(origin, 1 - my_y, core))

    def weights_cross(k, y):
        origin = lax.rem(my_z + k, z_size)
        wait_recv(x_hop(origin, y), False)
        start(c_hop(origin, y, core), False)

    def weights_ready():
        for origin in range(z_size):
            for y in range(2):
                for mine in (True, False):
                    wait_recv(c_hop(origin, y, 1 - core), mine)

    def weights_drain():
        for sign in (1, -1):
            for step in range(1, z_size):
                origin = my_z - sign * (step - 1)

                @pl.when(jnp.logical_and(on_line(origin), on_line(my_z + sign)))
                def _():
                    wait_send(z_hop(step, sign, origin, my_z + sign))

        for origin in range(z_size):
            wait_send(y_hop(origin, my_y))
            wait_send(x_hop(origin, 1 - my_y))
            for y in range(2):
                for mine in (True, False):
                    wait_send(c_hop(origin, y, core), mine)
        for k in range(1, z_size):
            wait_send(x_hop(lax.rem(my_z + k, z_size), my_y))

    for load in loads[:5]:
        load.wait()
    pl.semaphore_wait(barrier, n)
    weights_first()

    letters = lax.broadcasted_iota(jnp.int32, (emb_ref.shape[0], length), 0)
    for s in range(seqs):
        one_hot = jnp.where(tok_ref[s : s + 1, :] == letters, 1.0, 0.0).astype(BF)
        picked = lax.dot_general(one_hot, emb_ref[...], (((0,), (0,)), ((), ())), preferred_element_type=F32)
        x0_ref[s * length : (s + 1) * length, :] = (
            state_ref[s * length : (s + 1) * length, :].astype(F32) + picked
        )
    u1 = layer_norm(x0_ref[...]).astype(BF)
    for load in loads[5:]:
        load.wait()
    project_into(u1, wqkv_ref, qkv_ref, 256)
    low, high = half_masks(2 * head_size)

    def pair_cols(which, p):
        cols = pl.ds(pl.multiple_of(which * width + p * 2 * head_size, 2 * head_size), 2 * head_size)
        return [qkv_ref[pl.ds(s * length, length), cols] for s in range(seqs)]

    def scores(p, carry):
        q = pair_cols(0, p)
        k = jnp.concatenate(pair_cols(1, p), axis=1)
        for half, mask in ((0, low), (1, high)):
            part = dot_t(jnp.concatenate([x * mask for x in q], axis=1), k)
            part = part.astype(BF).reshape(chips, 2, share, length)
            for c in range(2):
                sbuf[c, :, 2 * p + half] = part[:, c]
        return carry

    lax.fori_loop(0, heads // 2, scores, 0)

    swap = pltpu.make_async_remote_copy(
        src_ref=sbuf.at[1 - core], dst_ref=rbuf, send_sem=pair_sems.at[0], recv_sem=pair_sems.at[1],
        device_id={"depth": sibling}, device_id_type=MESH,
    )
    swap.start()
    weights_step(1)
    swap.wait()

    def rs_y_copy(z):
        return pltpu.make_async_remote_copy(
            src_ref=tbuf.at[z_size + z], dst_ref=gbuf.at[z_size + z],
            send_sem=rs_send.at[z_size + z], recv_sem=rs_recv.at[z_size + z],
            device_id={"depth": place(my_z, 1 - my_y, core)}, device_id_type=MESH,
        )

    def rs_copy(k):
        return pltpu.make_async_remote_copy(
            src_ref=tbuf.at[k], dst_ref=gbuf.at[k], send_sem=rs_send.at[k], recv_sem=rs_recv.at[k],
            device_id={"depth": place(lax.rem(my_z + k, z_size), my_y, core)}, device_id_type=MESH,
        )

    def rs_y_start(k, carry):
        z = lax.rem(my_z + k, z_size)
        at = z * 2 + 1 - my_y
        tbuf[z_size + z] = (sbuf[core, at].astype(F32) + rbuf[at].astype(F32)).astype(BF)
        rs_y_copy(z).start()
        return carry

    lax.fori_loop(1, z_size + 1, rs_y_start, 0)

    def chips_sum(z):
        at = z * 2 + my_y
        rs_y_copy(z).wait_recv()
        return sbuf[core, at].astype(F32) + rbuf[at].astype(F32) + gbuf[z_size + z].astype(F32)

    def rs_start(k, carry):
        tbuf[k] = chips_sum(lax.rem(my_z + k, z_size)).astype(BF)
        rs_copy(k).start()
        return carry

    lax.fori_loop(1, z_size, rs_start, 0)
    weights_across(0)
    total = chips_sum(my_z)

    def rs_add(k, total):
        rs_copy(k).wait_recv()
        return total + gbuf[k].astype(F32)

    total = lax.fori_loop(1, z_size, rs_add, total)
    factor = 1.0 / (math.sqrt(head_size) * math.sqrt(seqs * n))
    spot = lax.broadcasted_iota(jnp.int32, (share, length), 1)
    row = lax.broadcasted_iota(jnp.int32, (share, length), 0) + me * share
    mine = jnp.sum(jnp.where(spot == row, chain_row[...], 0), axis=-1, keepdims=True)
    same = mine == chain_row[...]
    for h in range(heads):
        tied = total[h] * factor + jnp.where(same, bias_ref[1:2, h : h + 1], bias_ref[0:1, h : h + 1])
        top = jnp.max(tied, axis=-1, keepdims=True)
        weights = jnp.exp(tied - top)
        pbuf[me, h] = (weights / jnp.sum(weights, axis=-1, keepdims=True)).astype(BF)

    def ag_copy(k):
        return pltpu.make_async_remote_copy(
            src_ref=pbuf.at[me], dst_ref=pbuf.at[me], send_sem=ag_send.at[k], recv_sem=ag_recv.at[k],
            device_id={"depth": place(lax.rem(my_z + k, z_size), my_y, core)}, device_id_type=MESH,
        )

    def back(k):
        return lax.rem(my_z - k + z_size, z_size)

    def ag_y_copy(k):
        origin = place(back(k), my_y, core)
        return pltpu.make_async_remote_copy(
            src_ref=pbuf.at[origin], dst_ref=pbuf.at[origin],
            send_sem=ag_send.at[z_size + k], recv_sem=ag_recv.at[z_size + k],
            device_id={"depth": place(my_z, 1 - my_y, core)}, device_id_type=MESH,
        )

    def fw_copy(k, far):
        origin = place(back(k), 1 - my_y if far else my_y, core)
        at = z_size + k if far else k
        return pltpu.make_async_remote_copy(
            src_ref=pbuf.at[origin], dst_ref=pbuf.at[origin], send_sem=fw_send.at[at], recv_sem=fw_recv.at[at],
            device_id={"depth": sibling}, device_id_type=MESH,
        )

    def ag_start(k, carry):
        ag_copy(k).start()
        return carry

    lax.fori_loop(1, z_size, ag_start, 0)
    ag_y_copy(0).start()
    fw_copy(0, False).start()

    def ag_forward(k, carry):
        ag_copy(k).wait_recv()
        ag_y_copy(k).start()
        fw_copy(k, False).start()
        return carry

    lax.fori_loop(1, z_size, ag_forward, 0)
    for step in range(2, 3):
        weights_step(step)

    def ag_y_forward(k, carry):
        ag_y_copy(k).wait_recv()
        fw_copy(k, True).start()
        return carry

    lax.fori_loop(0, z_size, ag_y_forward, 0)

    def fw_wait(k, carry):
        fw_copy(k, False).wait_recv()
        fw_copy(k, True).wait_recv()
        return carry

    lax.fori_loop(0, z_size, fw_wait, 0)
    for step in range(3, z_size):
        weights_step(step)

    def mixing(p, carry):
        v = jnp.concatenate(pair_cols(2, p), axis=1)
        lows = jnp.concatenate([low] * seqs, axis=1)
        highs = jnp.concatenate([high] * seqs, axis=1)
        keys = jnp.concatenate([v * lows, v * highs], axis=0)
        probs = jnp.concatenate(
            [pbuf[:, 2 * p].reshape(length, length), pbuf[:, 2 * p + 1].reshape(length, length)], axis=1
        )
        mixed = dot(probs, keys).astype(BF)
        pair = 2 * head_size
        cols = pl.ds(pl.multiple_of(p * pair, pair), pair)
        for s in range(seqs):
            mix_ref[pl.ds(s * length, length), cols] = mixed[:, s * pair : (s + 1) * pair]
        return carry

    lax.fori_loop(0, heads // 2, mixing, 0)

    def finish(t, carry):
        cols = pl.ds(pl.multiple_of(t * 256, 256), 256)
        x1 = (x0_ref[:, cols] + dot(mix_ref[...], wo_ref[:, cols])).astype(BF)
        for s in range(seqs):
            xbuf[:, s, :, cols] = x1[s * length : (s + 1) * length].reshape(n, share, 256)
        return carry

    lax.fori_loop(0, width // 256, finish, 0)

    def aa_copy(k):
        other = lax.rem(me + k, n)
        return pltpu.make_async_remote_copy(
            src_ref=xbuf.at[other], dst_ref=block_ref.at[me], send_sem=aa_send.at[k], recv_sem=aa_recv.at[k],
            device_id={"depth": other}, device_id_type=MESH,
        )

    def aa_start(k, carry):
        aa_copy(k).start()
        return carry

    lax.fori_loop(1, n, aa_start, 0)
    keep = pltpu.make_async_copy(xbuf.at[me], block_ref.at[me], local_sem)
    keep.start()
    keep.wait()
    for k in range(1, z_size):
        weights_across(k)
    for k in range(1, z_size):
        weights_cross(k, my_y)

    def drain(k, carry):
        aa_copy(k).wait()
        return carry

    lax.fori_loop(1, n, drain, 0)

    def drain_sends(k, carry):
        rs_copy(k).wait_send()
        ag_copy(k).wait_send()
        return carry

    lax.fori_loop(1, z_size, drain_sends, 0)

    def drain_more(k, carry):
        rs_y_copy(k).wait_send()
        ag_y_copy(k).wait_send()
        fw_copy(k, False).wait_send()
        fw_copy(k, True).wait_send()
        return carry

    lax.fori_loop(0, z_size, drain_more, 0)

    def between():
        for k in range(z_size):
            weights_cross(k, 1 - my_y)

    rows = seqs * length
    all_seqs = seqs * n
    column_part(all_seqs, heads, head_size, block_ref, wqkv2_ref, wo2_ref, x0_ref, qkv_ref, mix_ref, between)
    weights_ready()
    u3 = layer_norm(x0_ref[...]).astype(BF)
    mix_ref[...] = u3
    feed_part(mix_ref, up_ref, down_ref, x0_ref)
    order = column_order(rows, all_seqs, share, True)
    out_ref[...] = dot(order, x0_ref[...].astype(BF)).astype(BF)
    weights_drain()


def column_order(rows, all_seqs, cols, inverse):
    r = lax.broadcasted_iota(jnp.int32, (rows, rows), 0)
    c = lax.broadcasted_iota(jnp.int32, (rows, rows), 1)
    if inverse:
        r, c = c, r
    return jnp.where(c == (r % all_seqs) * cols + r // all_seqs, 1.0, 0.0).astype(BF)


def column_part(all_seqs, heads, head_size, block_ref, wqkv_ref, wo_ref, flat_ref, qkv_ref, mix_ref, between):
    rows, width = flat_ref.shape
    cols = rows // all_seqs
    flat_ref[...] = dot(column_order(rows, all_seqs, cols, False), block_ref[...].reshape(rows, width))
    u2 = layer_norm(flat_ref[...]).astype(BF)
    project_into(u2, wqkv_ref, qkv_ref, 256)
    between()
    pair = 2 * head_size
    low, high = half_masks(pair)
    group = 128
    r = lax.broadcasted_iota(jnp.int32, (2 * group, group), 0)
    c = lax.broadcasted_iota(jnp.int32, (2 * group, group), 1)
    inside = (r % group) // all_seqs == c // all_seqs
    factor = 1.0 / math.sqrt(head_size)

    def attend(g, carry):
        here = pl.ds(pl.multiple_of(g * group, group), group)
        for p in range(heads // 2):
            q = qkv_ref[here, p * pair : (p + 1) * pair]
            k = qkv_ref[here, width + p * pair : width + (p + 1) * pair]
            v = qkv_ref[here, 2 * width + p * pair : 2 * width + (p + 1) * pair]
            scores = dot_t(jnp.concatenate([q * low, q * high], axis=0), k) * factor
            scores = jnp.where(inside, scores, -jnp.inf)
            top = jnp.max(scores, axis=-1, keepdims=True)
            weights = jnp.exp(scores - top)
            probs = (weights / jnp.sum(weights, axis=-1, keepdims=True)).astype(BF)
            probs = jnp.concatenate([probs[:group], probs[group:]], axis=1)
            values = jnp.concatenate([v * low, v * high], axis=0)
            mix_ref[here, p * pair : (p + 1) * pair] = dot(probs, values).astype(BF)
        return carry

    lax.fori_loop(0, rows // group, attend, 0)
    flat_ref[...] += dot(mix_ref[...], wo_ref[...])


def feed_part(u3_ref, up_ref, down_ref, acc_ref):
    n, up_rows, hidden_size = up_ref.shape
    down_rows, width = down_ref.shape[1:]
    span = max(d for d in range(1, n + 1) if n % d == 0 and d * down_rows <= 768)
    step = span * down_rows

    def body(t, carry):
        part = pl.ds(pl.multiple_of(t * step, step), step)
        pre = dot(u3_ref[...], up_ref[:, :, part].reshape(n * up_rows, step))
        hidden = (0.5 * pre * (1.0 + lax.erf(pre * math.sqrt(0.5)))).astype(BF)
        acc_ref[...] += dot(hidden, down_ref[pl.ds(t * span, span)].reshape(step, width))
        return carry

    lax.fori_loop(0, hidden_size // step, body, 0)


def fast_device(
    alignment_token_grid,
    residue_chain_index,
    alignment_state,
    embedding,
    chain_head_bias,
    row_query_key_value,
    row_output_weight,
    column_query_key_value,
    column_output_weight,
    feed_up_weight,
    feed_down_weight,
):
    seqs, length, width = alignment_state.shape
    heads = chain_head_bias.shape[1]
    head_size = width // heads
    n = lax.axis_size("depth")
    share = length // n
    rows = seqs * length
    all_seqs = seqs * n
    chunk = (heads, share, length)
    arrays = (
        alignment_token_grid,
        residue_chain_index.reshape(1, length),
        alignment_state.reshape(rows, width),
        embedding,
        chain_head_bias,
        row_query_key_value,
        row_output_weight,
        column_query_key_value,
        column_output_weight,
    )
    DMA = pltpu.SemaphoreType.DMA
    half = n // 2
    deep = n // 4
    result = pl.pallas_call(
        functools.partial(layer_kernel, n, seqs, length, heads, head_size),
        out_shape=jax.ShapeDtypeStruct((rows, width), BF),
        in_specs=[pl.BlockSpec(memory_space=pl.ANY)] * 11,
        out_specs=pl.BlockSpec(memory_space=pltpu.VMEM),
        scratch_shapes=[pltpu.VMEM(x.shape, x.dtype) for x in arrays]
        + [
            pltpu.VMEM((n,) + feed_up_weight.shape, BF),
            pltpu.VMEM((n,) + feed_down_weight.shape, BF),
            pltpu.VMEM((rows, width), F32),
            pltpu.VMEM((rows, 3 * width), BF),
            pltpu.VMEM((2, half) + chunk, BF),
            pltpu.VMEM((half,) + chunk, BF),
            pltpu.VMEM((half,) + chunk, BF),
            pltpu.VMEM((half,) + chunk, BF),
            pltpu.VMEM((n,) + chunk, BF),
            pltpu.VMEM((rows, width), BF),
            pltpu.VMEM((n, seqs, share, width), BF),
            pltpu.VMEM((n, seqs, share, width), BF),
            DMA((11,)), DMA((2,)),
            DMA((half,)), DMA((half,)), DMA((half,)), DMA((half,)),
            DMA((half,)), DMA((half,)), DMA((n,)), DMA((n,)), DMA,
            DMA((2, 2, deep)), DMA((2, 2, deep)), DMA((2, deep)), DMA((2, deep)),
            DMA((2, deep, 2)), DMA((2, deep, 2)), DMA((2, deep, 2)), DMA((2, deep, 2)),
        ],
        compiler_params=pltpu.CompilerParams(
            collective_id=0, has_side_effects=True, vmem_limit_bytes=58 * 2**20
        ),
        cost_estimate=pl.CostEstimate(
            flops=2 * rows * width * width * 18, bytes_accessed=40 * 2**20, transcendentals=0
        ),
        name="layer",
    )(*arrays, feed_up_weight, feed_down_weight)
    return result.reshape(all_seqs, share, width)


def layer_norm(values):
    center = values - jnp.mean(values, axis=-1, keepdims=True)
    spread = jnp.mean(center * center, axis=-1, keepdims=True)
    return center * lax.rsqrt(spread + 1e-05)


def chain_terms(query_ids, residue_chain_index, chain_head_bias):
    same = query_ids[:, None] == residue_chain_index[None, :]
    return jnp.where(
        same[:, None, :], chain_head_bias[1][None, :, None], chain_head_bias[0][None, :, None]
    )


def plain_device(
    alignment_token_grid,
    residue_chain_index,
    alignment_state,
    embedding,
    chain_head_bias,
    row_query_key_value,
    row_output_weight,
    column_query_key_value,
    column_output_weight,
    feed_up_weight,
    feed_down_weight,
):
    device_sequences = alignment_state.shape[0]
    residue_length = alignment_state.shape[1]
    hidden_width = alignment_state.shape[2]
    heads = chain_head_bias.shape[1]
    head_size = hidden_width // heads
    devices = lax.axis_size("depth")
    all_seqs = device_sequences * devices
    token_letters = embedding.shape[0]
    one_hot = (
        alignment_token_grid.reshape(-1)[:, None]
        == jnp.arange(token_letters, dtype=jnp.int32)[None, :]
    ).astype(jnp.bfloat16)
    initial_input0 = alignment_state.reshape(-1, hidden_width).astype(jnp.float32) + jnp.dot(
        one_hot, embedding, preferred_element_type=jnp.float32
    )
    u1 = layer_norm(initial_input0).astype(jnp.bfloat16)
    qkv1 = jnp.dot(u1, row_query_key_value, preferred_element_type=jnp.float32).astype(jnp.bfloat16)
    qkv1 = qkv1.reshape(device_sequences, residue_length, 3, heads, head_size)
    queries = qkv1[:, :, 0]
    keys_row = qkv1[:, :, 1]
    values_row = qkv1[:, :, 2]
    factor = 1.0 / (math.sqrt(head_size) * math.sqrt(all_seqs))
    partial_value = jnp.einsum(
        "sihd,sjhd->ihj", queries, keys_row, preferred_element_type=jnp.float32
    )
    tied = lax.psum(partial_value, "depth") * factor
    tied = tied + chain_terms(residue_chain_index, residue_chain_index, chain_head_bias)
    row_probs = jax.nn.softmax(tied, axis=-1).astype(jnp.bfloat16)
    row_mix = jnp.einsum(
        "ihj,sjhd->sihd", row_probs, values_row, preferred_element_type=jnp.float32
    ).astype(jnp.bfloat16)
    x1 = initial_input0 + jnp.dot(
        row_mix.reshape(-1, hidden_width), row_output_weight, preferred_element_type=jnp.float32
    )
    col_share = residue_length // devices
    x1 = x1.astype(jnp.bfloat16).reshape(device_sequences, devices, col_share, hidden_width)
    block = lax.all_to_all(x1, "depth", split_axis=1, concat_axis=0, tiled=True)
    seqs_here = block.shape[0]
    cols = block.shape[2]
    flat = block.reshape(seqs_here * cols, hidden_width).astype(jnp.float32)
    u2 = layer_norm(flat).astype(jnp.bfloat16)
    qkv2 = jnp.dot(u2, column_query_key_value, preferred_element_type=jnp.float32).astype(
        jnp.bfloat16
    )
    qkv2 = qkv2.reshape(seqs_here, cols, 3, heads, head_size)
    scores = jnp.einsum(
        "snhd,tnhd->nhst", qkv2[:, :, 0], qkv2[:, :, 1], preferred_element_type=jnp.float32
    ) / math.sqrt(head_size)
    col_probs = jax.nn.softmax(scores, axis=-1).astype(jnp.bfloat16)
    col_mix = jnp.einsum(
        "nhst,tnhd->snhd", col_probs, qkv2[:, :, 2], preferred_element_type=jnp.float32
    ).astype(jnp.bfloat16)
    result = flat + jnp.dot(
        col_mix.reshape(seqs_here * cols, hidden_width),
        column_output_weight,
        preferred_element_type=jnp.float32,
    )
    x2 = result.reshape(seqs_here, 1, cols, hidden_width)
    out_shape = (x2.shape[0], x2.shape[2], hidden_width)
    flat2 = x2.reshape(-1, hidden_width)
    u3 = layer_norm(flat2).astype(jnp.bfloat16)
    full_up, full_down = (
        lax.all_gather(feed_up_weight, "depth", axis=0, tiled=True),
        lax.all_gather(feed_down_weight, "depth", axis=0, tiled=True),
    )
    pre = jnp.dot(u3, full_up, preferred_element_type=jnp.float32)
    hidden = jax.nn.gelu(pre, approximate=False).astype(jnp.bfloat16)
    projected = jnp.dot(hidden, full_down, preferred_element_type=jnp.float32)
    return (flat2 + projected).astype(jnp.bfloat16).reshape(out_shape)


def per_device(*arrays):
    seqs, length, width = arrays[2].shape
    heads = arrays[4].shape[1]
    n = lax.axis_size("depth")
    fits = (
        n % 2 == 0
        and length % n == 0
        and (length // n) % 16 == 0
        and n % 4 == 0
        and n >= 16
        and lax.axis_size("groups") == 2
        and arrays[9].shape[0] % 16 == 0
        and arrays[10].shape[0] % 64 == 0
        and 128 % (seqs * n) == 0
        and (seqs * length) % 128 == 0
        and 2 * (width // heads) == 128
        and heads % 2 == 0
        and width % 256 == 0
    )
    return (fast_device if fits else plain_device)(*arrays)


def solution(mesh):
    in_specs = (
        P(("groups", "depth"), None),
        P("groups"),
        P(("groups", "depth"), None, None),
        P(),
        P(),
        P(),
        P(),
        P(),
        P(),
        P("depth", None),
        P("depth", None),
    )
    out_specs = P("groups", "depth", None)
    return jax.shard_map(
        per_device, mesh=mesh, in_specs=in_specs, out_specs=out_specs, check_vma=False
    )
```

```python
import functools
import math

import jax
import jax.numpy as jnp
from jax import lax
from jax.experimental import pallas as pl
from jax.experimental.pallas import tpu as pltpu
from jax.sharding import PartitionSpec as P

MESH = pl.DeviceIdType.MESH
BF = jnp.bfloat16
F32 = jnp.float32


def dot(a, b):
    return jnp.dot(a, b, preferred_element_type=F32)


def dot_t(a, b):
    return lax.dot_general(a, b, (((1,), (1,)), ((), ())), preferred_element_type=F32)


def half_masks(width):
    lane = lax.broadcasted_iota(jnp.int32, (1, width), 1)
    low = jnp.where(lane < width // 2, 1.0, 0.0)
    return low.astype(BF), (1.0 - low).astype(BF)


def project_into(source, weight_ref, target_ref, step):
    def body(t, carry):
        cols = pl.ds(pl.multiple_of(t * step, step), step)
        target_ref[:, cols] = dot(source, weight_ref[:, cols]).astype(BF)
        return carry

    lax.fori_loop(0, weight_ref.shape[1] // step, body, 0)


def layer_kernel(
    n, seqs, length, heads, head_size,
    tok_any, chain_any, state_any, emb_any, bias_any, wqkv_any, wo_any, wqkv2_any, wo2_any, up_any, down_any,
    out_ref,
    tok_ref, chain_row, state_ref, emb_ref, bias_ref, wqkv_ref, wo_ref, wqkv2_ref, wo2_ref, up_ref, down_ref,
    x0_ref, qkv_ref, sbuf, rbuf, tbuf, gbuf, pbuf, mix_ref, xbuf, block_ref,
    load_sems, pair_sems, rs_send, rs_recv, ag_send, ag_recv, fw_send, fw_recv, aa_send, aa_recv, local_sem,
    z_send, z_recv, y_send, y_recv, c_send, c_recv, x_send, x_recv,
):
    me = lax.axis_index("depth")
    core = lax.rem(me, 2)
    chip = me // 2
    chips = n // 2
    sibling = me + 1 - 2 * core
    share = length // n
    width = heads * head_size
    z_size = n // 4
    my_y = lax.rem(chip, 2)
    my_z = chip // 2
    group = lax.axis_index("groups")

    loads = [
        pltpu.make_async_copy(source, target, load_sems.at[k])
        for k, (source, target) in enumerate(
            (
                (up_any, up_ref.at[me]),
                (down_any, down_ref.at[me]),
                (tok_any, tok_ref),
                (emb_any, emb_ref),
                (state_any, state_ref),
                (chain_any, chain_row),
                (bias_any, bias_ref),
                (wqkv_any, wqkv_ref),
                (wo_any, wo_ref),
                (wqkv2_any, wqkv2_ref),
                (wo2_any, wo2_ref),
            )
        )
    ]
    for load in loads:
        load.start()

    barrier = pltpu.get_barrier_semaphore()

    def greet(k, carry):
        pl.semaphore_signal(
            barrier, inc=1, device_id={"depth": lax.rem(me + k, n)}, device_id_type=MESH
        )
        return carry

    lax.fori_loop(1, n, greet, 0)
    pl.semaphore_signal(barrier, inc=1, device_id={"groups": 1 - group}, device_id_type=MESH)

    def place(z, y, c):
        return (z * 2 + y) * 2 + c

    def hop(index, target, send, recv, at):
        return [
            pltpu.make_async_remote_copy(
                src_ref=ref.at[index], dst_ref=ref.at[index],
                send_sem=send.at[(w,) + at], recv_sem=recv.at[(w,) + at],
                device_id=target if isinstance(target, dict) else {"depth": target},
                device_id_type=MESH,
            )
            for w, ref in ((0, up_ref), (1, down_ref))
        ]

    def z_hop(step, sign, origin, target):
        return hop(place(origin, my_y, core), place(target, my_y, core), z_send, z_recv, (0 if sign > 0 else 1, step))

    def y_hop(origin, y):
        return hop(place(origin, y, core), place(my_z, 1 - my_y, core), y_send, y_recv, (origin,))

    def c_hop(origin, y, c):
        return hop(place(origin, y, c), sibling, c_send, c_recv, (origin, y))

    def x_hop(origin, y):
        return hop(place(origin, y, core), {"groups": 1 - group}, x_send, x_recv, (origin, y))

    def start(copies, mine=True):
        for w, copy in enumerate(copies):
            pl.when(group == (w if mine else 1 - w))(copy.start)

    def wait_recv(copies, mine=True):
        for w, copy in enumerate(copies):
            pl.when(group == (w if mine else 1 - w))(copy.wait_recv)

    def wait_send(copies, mine=True):
        for w, copy in enumerate(copies):
            pl.when(group == (w if mine else 1 - w))(copy.wait_send)

    def on_line(z):
        return jnp.logical_and(z >= 0, z < z_size)

    def weights_first():
        for sign in (1, -1):

            @pl.when(on_line(my_z + sign))
            def _():
                start(z_hop(1, sign, my_z, my_z + sign))

        start(y_hop(my_z, my_y))
        start(c_hop(my_z, my_y, core))
        start(c_hop(my_z, my_y, core), False)

    def weights_step(step):
        for sign in (1, -1):
            origin = my_z - sign * step

            @pl.when(on_line(origin))
            def _():
                wait_recv(z_hop(step, sign, origin, my_z))

                @pl.when(on_line(my_z + sign))
                def _():
                    start(z_hop(step + 1, sign, origin, my_z + sign))

                start(y_hop(origin, my_y))
                start(x_hop(origin, my_y))
                start(c_hop(origin, my_y, core))

    def weights_across(k):
        origin = lax.rem(my_z + k, z_size)
        wait_recv(y_hop(origin, 1 - my_y))
        start(x_hop(origin, 1 - my_y))
        start(c_hop(origin, 1 - my_y, core))

    def weights_cross(k, y):
        origin = lax.rem(my_z + k, z_size)
        wait_recv(x_hop(origin, y), False)
        start(c_hop(origin, y, core), False)

    def weights_ready():
        for origin in range(z_size):
            for y in range(2):
                for mine in (True, False):
                    wait_recv(c_hop(origin, y, 1 - core), mine)

    def weights_drain():
        for sign in (1, -1):
            for step in range(1, z_size):
                origin = my_z - sign * (step - 1)

                @pl.when(jnp.logical_and(on_line(origin), on_line(my_z + sign)))
                def _():
                    wait_send(z_hop(step, sign, origin, my_z + sign))

        for origin in range(z_size):
            wait_send(y_hop(origin, my_y))
            wait_send(x_hop(origin, 1 - my_y))
            for y in range(2):
                for mine in (True, False):
                    wait_send(c_hop(origin, y, core), mine)
        for k in range(1, z_size):
            wait_send(x_hop(lax.rem(my_z + k, z_size), my_y))

    for load in loads[:5]:
        load.wait()
    pl.semaphore_wait(barrier, n)
    weights_first()

    letters = lax.broadcasted_iota(jnp.int32, (emb_ref.shape[0], length), 0)
    for s in range(seqs):
        one_hot = jnp.where(tok_ref[s : s + 1, :] == letters, 1.0, 0.0).astype(BF)
        picked = lax.dot_general(one_hot, emb_ref[...], (((0,), (0,)), ((), ())), preferred_element_type=F32)
        x0_ref[s * length : (s + 1) * length, :] = (
            state_ref[s * length : (s + 1) * length, :].astype(F32) + picked
        )
    u1 = layer_norm(x0_ref[...]).astype(BF)
    for load in loads[5:]:
        load.wait()
    project_into(u1, wqkv_ref, qkv_ref, 256)
    low, high = half_masks(2 * head_size)

    def pair_cols(which, p):
        cols = pl.ds(pl.multiple_of(which * width + p * 2 * head_size, 2 * head_size), 2 * head_size)
        return [qkv_ref[pl.ds(s * length, length), cols] for s in range(seqs)]

    def scores(p, carry):
        q = pair_cols(0, p)
        k = jnp.concatenate(pair_cols(1, p), axis=1)
        for half, mask in ((0, low), (1, high)):
            part = dot_t(jnp.concatenate([x * mask for x in q], axis=1), k)
            part = part.astype(BF).reshape(chips, 2, share, length)
            for c in range(2):
                sbuf[c, :, 2 * p + half] = part[:, c]
        return carry

    lax.fori_loop(0, heads // 2, scores, 0)

    swap = pltpu.make_async_remote_copy(
        src_ref=sbuf.at[1 - core], dst_ref=rbuf, send_sem=pair_sems.at[0], recv_sem=pair_sems.at[1],
        device_id={"depth": sibling}, device_id_type=MESH,
    )
    swap.start()
    weights_step(1)
    swap.wait()

    def rs_y_copy(z):
        return pltpu.make_async_remote_copy(
            src_ref=tbuf.at[z_size + z], dst_ref=gbuf.at[z_size + z],
            send_sem=rs_send.at[z_size + z], recv_sem=rs_recv.at[z_size + z],
            device_id={"depth": place(my_z, 1 - my_y, core)}, device_id_type=MESH,
        )

    def rs_copy(k):
        return pltpu.make_async_remote_copy(
            src_ref=tbuf.at[k], dst_ref=gbuf.at[k], send_sem=rs_send.at[k], recv_sem=rs_recv.at[k],
            device_id={"depth": place(lax.rem(my_z + k, z_size), my_y, core)}, device_id_type=MESH,
        )

    def rs_y_start(k, carry):
        z = lax.rem(my_z + k, z_size)
        at = z * 2 + 1 - my_y
        tbuf[z_size + z] = (sbuf[core, at].astype(F32) + rbuf[at].astype(F32)).astype(BF)
        rs_y_copy(z).start()
        return carry

    lax.fori_loop(1, z_size + 1, rs_y_start, 0)

    def chips_sum(z):
        at = z * 2 + my_y
        rs_y_copy(z).wait_recv()
        return sbuf[core, at].astype(F32) + rbuf[at].astype(F32) + gbuf[z_size + z].astype(F32)

    def rs_start(k, carry):
        tbuf[k] = chips_sum(lax.rem(my_z + k, z_size)).astype(BF)
        rs_copy(k).start()
        return carry

    lax.fori_loop(1, z_size, rs_start, 0)
    weights_across(0)
    total = chips_sum(my_z)

    def rs_add(k, total):
        rs_copy(k).wait_recv()
        return total + gbuf[k].astype(F32)

    total = lax.fori_loop(1, z_size, rs_add, total)
    factor = 1.0 / (math.sqrt(head_size) * math.sqrt(seqs * n))
    spot = lax.broadcasted_iota(jnp.int32, (share, length), 1)
    row = lax.broadcasted_iota(jnp.int32, (share, length), 0) + me * share
    mine = jnp.sum(jnp.where(spot == row, chain_row[...], 0), axis=-1, keepdims=True)
    same = mine == chain_row[...]
    for h in range(heads):
        tied = total[h] * factor + jnp.where(same, bias_ref[1:2, h : h + 1], bias_ref[0:1, h : h + 1])
        top = jnp.max(tied, axis=-1, keepdims=True)
        weights = jnp.exp(tied - top)
        pbuf[me, h] = (weights / jnp.sum(weights, axis=-1, keepdims=True)).astype(BF)

    def ag_copy(k):
        return pltpu.make_async_remote_copy(
            src_ref=pbuf.at[me], dst_ref=pbuf.at[me], send_sem=ag_send.at[k], recv_sem=ag_recv.at[k],
            device_id={"depth": place(lax.rem(my_z + k, z_size), my_y, core)}, device_id_type=MESH,
        )

    def back(k):
        return lax.rem(my_z - k + z_size, z_size)

    def ag_y_copy(k):
        origin = place(back(k), my_y, core)
        return pltpu.make_async_remote_copy(
            src_ref=pbuf.at[origin], dst_ref=pbuf.at[origin],
            send_sem=ag_send.at[z_size + k], recv_sem=ag_recv.at[z_size + k],
            device_id={"depth": place(my_z, 1 - my_y, core)}, device_id_type=MESH,
        )

    def fw_copy(k, far):
        origin = place(back(k), 1 - my_y if far else my_y, core)
        at = z_size + k if far else k
        return pltpu.make_async_remote_copy(
            src_ref=pbuf.at[origin], dst_ref=pbuf.at[origin], send_sem=fw_send.at[at], recv_sem=fw_recv.at[at],
            device_id={"depth": sibling}, device_id_type=MESH,
        )

    def ag_start(k, carry):
        ag_copy(k).start()
        return carry

    lax.fori_loop(1, z_size, ag_start, 0)
    ag_y_copy(0).start()
    fw_copy(0, False).start()

    def ag_forward(k, carry):
        ag_copy(k).wait_recv()
        ag_y_copy(k).start()
        fw_copy(k, False).start()
        return carry

    lax.fori_loop(1, z_size, ag_forward, 0)
    for step in range(2, 3):
        weights_step(step)

    def ag_y_forward(k, carry):
        ag_y_copy(k).wait_recv()
        fw_copy(k, True).start()
        return carry

    lax.fori_loop(0, z_size, ag_y_forward, 0)

    def fw_wait(k, carry):
        fw_copy(k, False).wait_recv()
        fw_copy(k, True).wait_recv()
        return carry

    lax.fori_loop(0, z_size, fw_wait, 0)
    for step in range(3, z_size):
        weights_step(step)

    def mixing(p, carry):
        v = jnp.concatenate(pair_cols(2, p), axis=1)
        lows = jnp.concatenate([low] * seqs, axis=1)
        highs = jnp.concatenate([high] * seqs, axis=1)
        keys = jnp.concatenate([v * lows, v * highs], axis=0)
        probs = jnp.concatenate(
            [pbuf[:, 2 * p].reshape(length, length), pbuf[:, 2 * p + 1].reshape(length, length)], axis=1
        )
        mixed = dot(probs, keys).astype(BF)
        pair = 2 * head_size
        cols = pl.ds(pl.multiple_of(p * pair, pair), pair)
        for s in range(seqs):
            mix_ref[pl.ds(s * length, length), cols] = mixed[:, s * pair : (s + 1) * pair]
        return carry

    lax.fori_loop(0, heads // 2, mixing, 0)

    def finish(t, carry):
        cols = pl.ds(pl.multiple_of(t * 256, 256), 256)
        x1 = (x0_ref[:, cols] + dot(mix_ref[...], wo_ref[:, cols])).astype(BF)
        for s in range(seqs):
            xbuf[:, s, :, cols] = x1[s * length : (s + 1) * length].reshape(n, share, 256)
        return carry

    lax.fori_loop(0, width // 256, finish, 0)

    def aa_copy(k):
        other = lax.rem(me + k, n)
        return pltpu.make_async_remote_copy(
            src_ref=xbuf.at[other], dst_ref=block_ref.at[me], send_sem=aa_send.at[k], recv_sem=aa_recv.at[k],
            device_id={"depth": other}, device_id_type=MESH,
        )

    def aa_start(k, carry):
        aa_copy(k).start()
        return carry

    lax.fori_loop(1, n, aa_start, 0)
    keep = pltpu.make_async_copy(xbuf.at[me], block_ref.at[me], local_sem)
    keep.start()
    keep.wait()
    for k in range(1, z_size):
        weights_across(k)

    def drain(k, carry):
        aa_copy(k).wait()
        return carry

    lax.fori_loop(1, n, drain, 0)

    def drain_sends(k, carry):
        rs_copy(k).wait_send()
        ag_copy(k).wait_send()
        return carry

    lax.fori_loop(1, z_size, drain_sends, 0)

    def drain_more(k, carry):
        rs_y_copy(k).wait_send()
        ag_y_copy(k).wait_send()
        fw_copy(k, False).wait_send()
        fw_copy(k, True).wait_send()
        return carry

    lax.fori_loop(0, z_size, drain_more, 0)

    def between():
        for k in range(1, z_size):
            weights_cross(k, my_y)
        for k in range(z_size):
            weights_cross(k, 1 - my_y)

    rows = seqs * length
    all_seqs = seqs * n
    column_part(all_seqs, heads, head_size, block_ref, wqkv2_ref, wo2_ref, x0_ref, qkv_ref, mix_ref, between)
    weights_ready()
    u3 = layer_norm(x0_ref[...]).astype(BF)
    mix_ref[...] = u3
    feed_part(mix_ref, up_ref, down_ref, x0_ref)
    order = column_order(rows, all_seqs, share, True)
    out_ref[...] = dot(order, x0_ref[...].astype(BF)).astype(BF)
    weights_drain()


def column_order(rows, all_seqs, cols, inverse):
    r = lax.broadcasted_iota(jnp.int32, (rows, rows), 0)
    c = lax.broadcasted_iota(jnp.int32, (rows, rows), 1)
    if inverse:
        r, c = c, r
    return jnp.where(c == (r % all_seqs) * cols + r // all_seqs, 1.0, 0.0).astype(BF)


def column_part(all_seqs, heads, head_size, block_ref, wqkv_ref, wo_ref, flat_ref, qkv_ref, mix_ref, between):
    rows, width = flat_ref.shape
    cols = rows // all_seqs
    flat_ref[...] = dot(column_order(rows, all_seqs, cols, False), block_ref[...].reshape(rows, width))
    u2 = layer_norm(flat_ref[...]).astype(BF)
    project_into(u2, wqkv_ref, qkv_ref, 256)
    between()
    pair = 2 * head_size
    low, high = half_masks(pair)
    group = 128
    r = lax.broadcasted_iota(jnp.int32, (2 * group, group), 0)
    c = lax.broadcasted_iota(jnp.int32, (2 * group, group), 1)
    inside = (r % group) // all_seqs == c // all_seqs
    factor = 1.0 / math.sqrt(head_size)

    def attend(g, carry):
        here = pl.ds(pl.multiple_of(g * group, group), group)
        for p in range(heads // 2):
            q = qkv_ref[here, p * pair : (p + 1) * pair]
            k = qkv_ref[here, width + p * pair : width + (p + 1) * pair]
            v = qkv_ref[here, 2 * width + p * pair : 2 * width + (p + 1) * pair]
            scores = dot_t(jnp.concatenate([q * low, q * high], axis=0), k) * factor
            scores = jnp.where(inside, scores, -jnp.inf)
            top = jnp.max(scores, axis=-1, keepdims=True)
            weights = jnp.exp(scores - top)
            probs = (weights / jnp.sum(weights, axis=-1, keepdims=True)).astype(BF)
            probs = jnp.concatenate([probs[:group], probs[group:]], axis=1)
            values = jnp.concatenate([v * low, v * high], axis=0)
            mix_ref[here, p * pair : (p + 1) * pair] = dot(probs, values).astype(BF)
        return carry

    lax.fori_loop(0, rows // group, attend, 0)
    flat_ref[...] += dot(mix_ref[...], wo_ref[...])


def feed_part(u3_ref, up_ref, down_ref, acc_ref):
    n, up_rows, hidden_size = up_ref.shape
    down_rows, width = down_ref.shape[1:]
    span = max(d for d in range(1, n + 1) if n % d == 0 and d * down_rows <= 768)
    step = span * down_rows

    def body(t, carry):
        part = pl.ds(pl.multiple_of(t * step, step), step)
        pre = dot(u3_ref[...], up_ref[:, :, part].reshape(n * up_rows, step))
        hidden = (0.5 * pre * (1.0 + lax.erf(pre * math.sqrt(0.5)))).astype(BF)
        acc_ref[...] += dot(hidden, down_ref[pl.ds(t * span, span)].reshape(step, width))
        return carry

    lax.fori_loop(0, hidden_size // step, body, 0)


def fast_device(
    alignment_token_grid,
    residue_chain_index,
    alignment_state,
    embedding,
    chain_head_bias,
    row_query_key_value,
    row_output_weight,
    column_query_key_value,
    column_output_weight,
    feed_up_weight,
    feed_down_weight,
):
    seqs, length, width = alignment_state.shape
    heads = chain_head_bias.shape[1]
    head_size = width // heads
    n = lax.axis_size("depth")
    share = length // n
    rows = seqs * length
    all_seqs = seqs * n
    chunk = (heads, share, length)
    arrays = (
        alignment_token_grid,
        residue_chain_index.reshape(1, length),
        alignment_state.reshape(rows, width),
        embedding,
        chain_head_bias,
        row_query_key_value,
        row_output_weight,
        column_query_key_value,
        column_output_weight,
    )
    DMA = pltpu.SemaphoreType.DMA
    half = n // 2
    deep = n // 4
    result = pl.pallas_call(
        functools.partial(layer_kernel, n, seqs, length, heads, head_size),
        out_shape=jax.ShapeDtypeStruct((rows, width), BF),
        in_specs=[pl.BlockSpec(memory_space=pl.ANY)] * 11,
        out_specs=pl.BlockSpec(memory_space=pltpu.VMEM),
        scratch_shapes=[pltpu.VMEM(x.shape, x.dtype) for x in arrays]
        + [
            pltpu.VMEM((n,) + feed_up_weight.shape, BF),
            pltpu.VMEM((n,) + feed_down_weight.shape, BF),
            pltpu.VMEM((rows, width), F32),
            pltpu.VMEM((rows, 3 * width), BF),
            pltpu.VMEM((2, half) + chunk, BF),
            pltpu.VMEM((half,) + chunk, BF),
            pltpu.VMEM((half,) + chunk, BF),
            pltpu.VMEM((half,) + chunk, BF),
            pltpu.VMEM((n,) + chunk, BF),
            pltpu.VMEM((rows, width), BF),
            pltpu.VMEM((n, seqs, share, width), BF),
            pltpu.VMEM((n, seqs, share, width), BF),
            DMA((11,)), DMA((2,)),
            DMA((half,)), DMA((half,)), DMA((half,)), DMA((half,)),
            DMA((half,)), DMA((half,)), DMA((n,)), DMA((n,)), DMA,
            DMA((2, 2, deep)), DMA((2, 2, deep)), DMA((2, deep)), DMA((2, deep)),
            DMA((2, deep, 2)), DMA((2, deep, 2)), DMA((2, deep, 2)), DMA((2, deep, 2)),
        ],
        compiler_params=pltpu.CompilerParams(
            collective_id=0, has_side_effects=True, vmem_limit_bytes=58 * 2**20
        ),
        cost_estimate=pl.CostEstimate(
            flops=2 * rows * width * width * 18, bytes_accessed=40 * 2**20, transcendentals=0
        ),
        name="layer",
    )(*arrays, feed_up_weight, feed_down_weight)
    return result.reshape(all_seqs, share, width)


def layer_norm(values):
    center = values - jnp.mean(values, axis=-1, keepdims=True)
    spread = jnp.mean(center * center, axis=-1, keepdims=True)
    return center * lax.rsqrt(spread + 1e-05)


def chain_terms(query_ids, residue_chain_index, chain_head_bias):
    same = query_ids[:, None] == residue_chain_index[None, :]
    return jnp.where(
        same[:, None, :], chain_head_bias[1][None, :, None], chain_head_bias[0][None, :, None]
    )


def plain_device(
    alignment_token_grid,
    residue_chain_index,
    alignment_state,
    embedding,
    chain_head_bias,
    row_query_key_value,
    row_output_weight,
    column_query_key_value,
    column_output_weight,
    feed_up_weight,
    feed_down_weight,
):
    device_sequences = alignment_state.shape[0]
    residue_length = alignment_state.shape[1]
    hidden_width = alignment_state.shape[2]
    heads = chain_head_bias.shape[1]
    head_size = hidden_width // heads
    devices = lax.axis_size("depth")
    all_seqs = device_sequences * devices
    token_letters = embedding.shape[0]
    one_hot = (
        alignment_token_grid.reshape(-1)[:, None]
        == jnp.arange(token_letters, dtype=jnp.int32)[None, :]
    ).astype(jnp.bfloat16)
    initial_input0 = alignment_state.reshape(-1, hidden_width).astype(jnp.float32) + jnp.dot(
        one_hot, embedding, preferred_element_type=jnp.float32
    )
    u1 = layer_norm(initial_input0).astype(jnp.bfloat16)
    qkv1 = jnp.dot(u1, row_query_key_value, preferred_element_type=jnp.float32).astype(jnp.bfloat16)
    qkv1 = qkv1.reshape(device_sequences, residue_length, 3, heads, head_size)
    queries = qkv1[:, :, 0]
    keys_row = qkv1[:, :, 1]
    values_row = qkv1[:, :, 2]
    factor = 1.0 / (math.sqrt(head_size) * math.sqrt(all_seqs))
    partial_value = jnp.einsum(
        "sihd,sjhd->ihj", queries, keys_row, preferred_element_type=jnp.float32
    )
    tied = lax.psum(partial_value, "depth") * factor
    tied = tied + chain_terms(residue_chain_index, residue_chain_index, chain_head_bias)
    row_probs = jax.nn.softmax(tied, axis=-1).astype(jnp.bfloat16)
    row_mix = jnp.einsum(
        "ihj,sjhd->sihd", row_probs, values_row, preferred_element_type=jnp.float32
    ).astype(jnp.bfloat16)
    x1 = initial_input0 + jnp.dot(
        row_mix.reshape(-1, hidden_width), row_output_weight, preferred_element_type=jnp.float32
    )
    col_share = residue_length // devices
    x1 = x1.astype(jnp.bfloat16).reshape(device_sequences, devices, col_share, hidden_width)
    block = lax.all_to_all(x1, "depth", split_axis=1, concat_axis=0, tiled=True)
    seqs_here = block.shape[0]
    cols = block.shape[2]
    flat = block.reshape(seqs_here * cols, hidden_width).astype(jnp.float32)
    u2 = layer_norm(flat).astype(jnp.bfloat16)
    qkv2 = jnp.dot(u2, column_query_key_value, preferred_element_type=jnp.float32).astype(
        jnp.bfloat16
    )
    qkv2 = qkv2.reshape(seqs_here, cols, 3, heads, head_size)
    scores = jnp.einsum(
        "snhd,tnhd->nhst", qkv2[:, :, 0], qkv2[:, :, 1], preferred_element_type=jnp.float32
    ) / math.sqrt(head_size)
    col_probs = jax.nn.softmax(scores, axis=-1).astype(jnp.bfloat16)
    col_mix = jnp.einsum(
        "nhst,tnhd->snhd", col_probs, qkv2[:, :, 2], preferred_element_type=jnp.float32
    ).astype(jnp.bfloat16)
    result = flat + jnp.dot(
        col_mix.reshape(seqs_here * cols, hidden_width),
        column_output_weight,
        preferred_element_type=jnp.float32,
    )
    x2 = result.reshape(seqs_here, 1, cols, hidden_width)
    out_shape = (x2.shape[0], x2.shape[2], hidden_width)
    flat2 = x2.reshape(-1, hidden_width)
    u3 = layer_norm(flat2).astype(jnp.bfloat16)
    full_up, full_down = (
        lax.all_gather(feed_up_weight, "depth", axis=0, tiled=True),
        lax.all_gather(feed_down_weight, "depth", axis=0, tiled=True),
    )
    pre = jnp.dot(u3, full_up, preferred_element_type=jnp.float32)
    hidden = jax.nn.gelu(pre, approximate=False).astype(jnp.bfloat16)
    projected = jnp.dot(hidden, full_down, preferred_element_type=jnp.float32)
    return (flat2 + projected).astype(jnp.bfloat16).reshape(out_shape)


def per_device(*arrays):
    seqs, length, width = arrays[2].shape
    heads = arrays[4].shape[1]
    n = lax.axis_size("depth")
    fits = (
        n % 2 == 0
        and length % n == 0
        and (length // n) % 16 == 0
        and n % 4 == 0
        and n >= 16
        and lax.axis_size("groups") == 2
        and arrays[9].shape[0] % 16 == 0
        and arrays[10].shape[0] % 64 == 0
        and 128 % (seqs * n) == 0
        and (seqs * length) % 128 == 0
        and 2 * (width // heads) == 128
        and heads % 2 == 0
        and width % 256 == 0
    )
    return (fast_device if fits else plain_device)(*arrays)


def solution(mesh):
    in_specs = (
        P(("groups", "depth"), None),
        P("groups"),
        P(("groups", "depth"), None, None),
        P(),
        P(),
        P(),
        P(),
        P(),
        P(),
        P("depth", None),
        P("depth", None),
    )
    out_specs = P("groups", "depth", None)
    return jax.shard_map(
        per_device, mesh=mesh, in_specs=in_specs, out_specs=out_specs, check_vma=False
    )
```
